32 devices in a mesh: groups: 2 (over y), space: 4 (over z), clus: 4 (over x, core).
Axes of the slice: x: 2, y: 2, z: 4, core: 2. Of those that a mesh axis runs over, the one named last changes fastest.
Arguments:
- snapshots: bfloat16 [256, 5, 49152], P('groups', None, ('space', 'clus')), parts along dimension 0
- labels: int32 [256], P('groups'), parts along dimension 0, may hold values from 0 to 3, as said below
- start: float32 [256, 16], P('groups'), parts along dimension 0, may hold values from -6 to 6
- successor: int32 [8], P('groups'), parts along dimension 0, may hold values from 0 to 3, as said below
Outputs:
- modes: bfloat16 [8, 16, 5, 49152], P(('groups', 'clus'), None, None, 'space'), parts along dimension 0
- coefficients: float32 [256, 16], P(('groups', 'clus')), parts along dimension 0
- correlations: float32 [8, 16, 16], P(('groups', 'clus')), parts along dimension 0
The draws below stay inside these ranges and needn't reach their ends.
There are 2 independent parts, one for each index of `groups`. The reference program is written for one: setup_inputs(seed, part) draws one part's arguments, and reference() takes and returns one part's arrays. A program takes and returns all parts, laid end to end along the dimension named above; each array names one. Nothing has to cross between parts.
Inputs may be any that keep to these rules, and one draw needn't show every extreme that they name: `labels`: of the 32 snapshots of each aligned block (those of one index of clus), every cluster holds at least 6 and at most 8; in every block some cluster holds exactly 8. Following successor from any cluster visits all 4 clusters once before returning.
All inputs are finite; a program needn't handle non-finite values.
Results may differ from the reference program's by a relative error of at most 0.0045.
Values may be sent and summed in bfloat16 or wider, within the bound.
A program may use at most 64 MiB of HBM per device.

```python
import jax
import jax.numpy as jnp
from jax import lax

VARS = 5
MODES = 16
ITERS = 2
SNAP_DEV = 32
K = 4
NSNAP = 128
NCELLS = 49152
CAP = 8
BASE = 6
N_SPACE = 4
N_CLUS = 4


strengths = (0.7, 0.6, 0.55, 0.5, 0.45, 0.4, 0.4, 0.35, 0.35, 0.3, 0.3, 0.25)


def draw_snapshots(key, part):
    keys = jax.random.split(key, 6)
    noise = jax.random.normal(keys[0], (NSNAP, VARS, NCELLS), jnp.float32)
    lagged = jnp.roll(noise, 1, axis=0)
    lag_weight = 0.6 * jax.random.normal(keys[1], (NSNAP, 1, 1), jnp.float32)
    pattern_keys = jax.random.split(keys[2], len(strengths))
    weight_keys = jax.random.split(keys[3], len(strengths))
    shared = jnp.zeros((NSNAP, VARS, NCELLS), jnp.float32)
    for position in range(len(strengths)):
        pattern = jax.random.uniform(pattern_keys[position], (1, VARS, NCELLS), jnp.float32, -1.5, 1.5)
        weight = jax.random.normal(weight_keys[position], (NSNAP, 1, 1), jnp.float32)
        shared = shared + strengths[position] * weight * pattern
    scale = jnp.exp(jax.random.uniform(keys[5], (NSNAP, 1, 1), jnp.float32, -0.5, 0.5))
    values = scale * (noise + lag_weight * lagged + shared)
    return values.astype(jnp.bfloat16)


def draw_labels(key, part):
    blocks = NSNAP // SNAP_DEV
    order = jax.random.permutation(jax.random.fold_in(key, 11), K)
    rest_count = SNAP_DEV - BASE * K - (CAP - BASE)

    def one_block(index):
        block_key = jax.random.fold_in(key, 100 + index)
        pick = jax.random.randint(jax.random.fold_in(block_key, 1), (), 0, max(K // 2, 1))
        hot = order[pick].astype(jnp.int32)
        offset = jax.random.randint(jax.random.fold_in(block_key, 2), (), 0, K - 1)
        base_part = jnp.repeat(jnp.arange(K, dtype=jnp.int32), BASE)
        hot_part = jnp.full((CAP - BASE,), 1, jnp.int32) * hot
        rest_part = (hot + 1 + (jnp.arange(rest_count, dtype=jnp.int32) + offset) % (K - 1)) % K
        joined = jnp.concatenate([base_part, hot_part, rest_part.astype(jnp.int32)])
        shuffle = jax.random.permutation(jax.random.fold_in(block_key, 3), SNAP_DEV)
        return joined[shuffle]
    return jax.vmap(one_block)(jnp.arange(blocks, dtype=jnp.int32)).reshape(NSNAP).astype(jnp.int32)


def draw_successor(key, part):
    order = jax.random.permutation(jax.random.fold_in(key, 5), K).astype(jnp.int32)
    return jnp.zeros((K,), jnp.int32).at[order].set(jnp.roll(order, -1))


def normal_values(rng, shape, scale, most, kind=jnp.bfloat16):
    values = jax.random.normal(rng, shape, jnp.float32) * scale
    return jnp.minimum(jnp.maximum(values, -most), most).astype(kind)


def setup_inputs(seed: int = 0, part: int = 0) -> dict:
    key_list = jax.random.split(jax.random.key(seed), 5)
    part_splits = jax.random.split(jax.random.fold_in(key_list[4], part), 5)
    snapshots = draw_snapshots(jax.random.fold_in(jax.random.fold_in(key_list[4], part), 71), part)
    labels = draw_labels(jax.random.fold_in(jax.random.fold_in(key_list[4], part), 71), part)
    start = normal_values(part_splits[2], (NSNAP, MODES), 1.0, 6.0, jnp.float32)
    successor = draw_successor(jax.random.fold_in(jax.random.fold_in(key_list[4], part), 71), part)
    return dict(snapshots=snapshots, labels=labels, start=start, successor=successor)


def subspace(gram, member, start):
    basis = member[:, :, None] * start[None, :, :]
    for step in range(ITERS):
        image = member[:, :, None] * jnp.einsum('st,ktm->ksm', gram, basis, precision=lax.Precision.HIGHEST) + basis
        inner = jnp.einsum('ksm,ksn->kmn', image, image, precision=lax.Precision.HIGHEST)
        lower = jnp.linalg.cholesky(inner)
        basis = lax.linalg.triangular_solve(lower, image, left_side=False, lower=True, transpose_a=True)
    return basis

def reference(snapshots, labels, start, successor):
    count, variables, cells = snapshots.shape
    blocks = N_SPACE * N_CLUS
    width = cells // blocks
    clusters = N_CLUS

    def block_gram(total, index):
        piece = lax.dynamic_slice_in_dim(snapshots, index * width, width, 2).reshape(count, variables * width).astype(jnp.float32)
        return (total + jnp.dot(piece, piece.T, precision=lax.Precision.HIGHEST), None)
    total, unused = lax.scan(block_gram, jnp.zeros((count, count), jnp.float32), jnp.arange(blocks, dtype=jnp.int32))
    gram = total / (variables * cells)
    member = (labels[None, :] == jnp.arange(clusters, dtype=jnp.int32)[:, None]).astype(jnp.float32)
    basis = subspace(gram, member, start)
    coefficients = basis[labels, jnp.arange(count, dtype=jnp.int32)]
    rounded = basis.astype(jnp.bfloat16)
    wide = rounded.astype(jnp.float32)
    left = jnp.transpose(wide, (0, 2, 1)).reshape(clusters * MODES, count)

    def block_modes(index):
        piece = lax.dynamic_slice_in_dim(snapshots, index * width, width, 2).reshape(count, variables * width).astype(jnp.float32)
        return jnp.dot(left, piece, precision=lax.Precision.HIGHEST).astype(jnp.bfloat16).reshape(clusters, MODES, variables, width)
    stacked = lax.map(block_modes, jnp.arange(blocks, dtype=jnp.int32))
    modes = jnp.transpose(stacked, (1, 2, 3, 0, 4)).reshape(clusters, MODES, variables, cells)
    partner = wide[successor]
    image = jnp.einsum('st,atn->asn', gram, partner, precision=lax.Precision.HIGHEST)
    correlations = jnp.einsum('asm,asn->amn', wide, image, precision=lax.Precision.HIGHEST)
    return (modes, coefficients, correlations)
```

```python
import functools

import jax
import jax.numpy as jnp
from jax import lax
from jax.experimental import pallas as pl
from jax.experimental.pallas import tpu as pltpu
from jax.sharding import PartitionSpec as P

ITERS = 2
TILE = 8
MESH = pl.DeviceIdType.MESH


def split3(x):
    high = x.astype(jnp.bfloat16)
    rest = x - high.astype(jnp.float32)
    middle = rest.astype(jnp.bfloat16)
    low = (rest - middle.astype(jnp.float32)).astype(jnp.bfloat16)
    return high, middle, low


def dot(a, b):
    return jnp.dot(a, b, preferred_element_type=jnp.float32)


def times_gram(rows, pieces, count):
    modes = rows.shape[0]
    parts = dot(jnp.concatenate(split3(rows), axis=0), pieces)
    high = parts[:modes]
    middle = parts[modes : 2 * modes, : 2 * count]
    low = parts[2 * modes :, :count]
    return (
        (high[:, 2 * count :] + middle[:, count:] + low)
        + (high[:, count : 2 * count] + middle[:, :count])
        + high[:, :count]
    )


def orthonormal(rows, same):
    modes, count = rows.shape
    half = modes // 2
    first = [0 if j < half else half for j in range(modes)]
    pairs = jnp.concatenate([rows[j : j + 1] * rows[first[j] :] for j in range(modes)], axis=0)
    total = pairs.shape[0]
    sums = dot(jnp.concatenate(split3(pairs), axis=0), same)
    inner = sums[2 * total :] + sums[total : 2 * total] + sums[:total]
    columns = []
    at = 0
    for j in range(modes):
        height = modes - first[j]
        columns.append(inner[at : at + height])
        at += height
    index = lax.broadcasted_iota(jnp.int32, (modes, count), 0)
    result = jnp.zeros_like(rows)
    rest = rows
    for j in range(modes):
        here = j - first[j]
        scale = lax.rsqrt(columns[j][here : here + 1])
        lower = columns[j] * scale
        solved = rest[j - (modes - rest.shape[0]) :][:1] * scale
        result = jnp.where(index == j, solved, result)
        if j == modes - 1:
            break
        if first[j + 1] != first[j]:
            lower = lower[half:]
            rest = rest[half:]
            shift = half
        else:
            shift = first[j]
        rest = rest - lower * solved
        for n in range(j + 1, modes):
            factor = lower[n - shift : n - shift + 1]
            columns[n] = columns[n] - (lower if first[n] == shift else lower[half:]) * factor
    return result


def kernel(
    sizes,
    snap_hbm,
    labels_ref,
    start_ref,
    succ_ref,
    modes_ref,
    coef_ref,
    corr_ref,
    snap,
    partial,
    landed,
    chunk,
    gram,
    stage,
    load_sem,
    rs_send,
    rs_recv,
    ag_send,
    ag_recv,
    out_send,
    out_recv,
    own_sem,
):
    spaces, clusters = sizes
    variables, count, width = snap.shape
    modes = start_ref.shape[0]
    devices = spaces * clusters
    reducers = count // TILE if devices > count // TILE else devices
    tall = count // reducers
    owner = lax.axis_index("clus")
    me = lax.axis_index("space") * clusters + owner

    def place(index):
        return {"space": index // clusters, "clus": index % clusters}

    def when(condition, body):
        if reducers == devices:
            body()
        else:
            pl.when(condition)(body)

    def load(v):
        return pltpu.make_async_copy(snap_hbm.at[v], snap.at[v], load_sem.at[v])

    for v in range(variables):
        load(v).start()
    barrier = pltpu.get_barrier_semaphore()

    @pl.loop(1, devices)
    def _(d):
        target = lax.rem(me + d, devices)
        pl.semaphore_signal(barrier, inc=1, device_id=place(target), device_id_type=MESH)

    partial[...] = jnp.zeros_like(partial)

    @pl.loop(0, variables)
    def _(v):
        load(v).wait()
        block = snap[v]
        partial[...] += lax.dot_general(
            block, block, (((1,), (1,)), ((), ())), preferred_element_type=jnp.float32
        )

    pl.semaphore_wait(barrier, devices - 1)

    def part_copy(d):
        target = lax.rem(me + d, devices)
        rows = pl.ds(pl.multiple_of(target * tall, tall), tall)
        return target, pltpu.make_async_remote_copy(
            src_ref=partial.at[rows],
            dst_ref=landed.at[d],
            send_sem=rs_send.at[d],
            recv_sem=rs_recv.at[d],
            device_id=place(target),
            device_id_type=MESH,
        )

    def sum_copy(d):
        target = lax.rem(me + d, devices)
        rows = pl.ds(pl.multiple_of(me * tall, tall), tall)
        return pltpu.make_async_remote_copy(
            src_ref=chunk,
            dst_ref=gram.at[rows],
            send_sem=ag_send.at[d],
            recv_sem=ag_recv.at[d],
            device_id=place(target),
            device_id_type=MESH,
        )

    @pl.loop(1, devices)
    def _(d):
        target = lax.rem(me + d, devices)
        when(target < reducers, lambda: part_copy(d)[1].start())

    label_row = labels_ref[...]
    wide = jnp.broadcast_to(label_row.astype(jnp.float32), (count, count))
    same = (wide == wide.T).astype(jnp.bfloat16)

    def reduce():
        own = pl.ds(pl.multiple_of(me * tall, tall), tall)

        def add(d, total):
            part_copy(d)[1].wait_recv()
            return total + landed[d]

        total = lax.fori_loop(1, devices, add, partial[own])
        total = total * (1.0 / (variables * width * devices))
        chunk[...] = total
        gram[own] = total

        @pl.loop(1, devices)
        def _(d):
            sum_copy(d).start()

    when(me < reducers, reduce)

    @pl.loop(1, devices)
    def _(d):
        source = lax.rem(me + devices - d, devices)
        when(source < reducers, lambda: sum_copy(d).wait_recv())

    pieces = split3(gram[...])
    masked = jnp.concatenate([same * piece for piece in pieces], axis=1)
    basis = start_ref[...]
    for step in range(ITERS):
        image = times_gram(basis, masked, count) + basis
        basis = orthonormal(image, same)

    rounded = basis.astype(jnp.bfloat16)
    keep = basis.astype(jnp.bfloat16).astype(jnp.float32)
    left = jnp.concatenate(
        [jnp.where(label_row == k, keep, 0.0) for k in range(clusters)], axis=0
    ).astype(jnp.bfloat16)

    def mode_copy(v, d):
        target = lax.rem(owner + d, clusters)
        return pltpu.make_async_remote_copy(
            src_ref=stage.at[target, v],
            dst_ref=modes_ref.at[v, :, pl.ds(pl.multiple_of(owner * width, width), width)],
            send_sem=out_send.at[v, d],
            recv_sem=out_recv.at[v, d],
            device_id={"clus": target},
            device_id_type=MESH,
        )

    def own_copy(v):
        return pltpu.make_async_copy(
            stage.at[owner, v],
            modes_ref.at[v, :, pl.ds(pl.multiple_of(owner * width, width), width)],
            own_sem.at[v],
        )

    step = width // 3 if width % 384 == 0 else width

    @pl.loop(0, variables)
    def _(v):
        @pl.loop(0, width // step)
        def _(c):
            cells = pl.ds(pl.multiple_of(c * step, step), step)
            made = dot(left, snap[v, :, cells]).astype(jnp.bfloat16)
            for k in range(clusters):
                stage[k, v, :, cells] = made[k * modes : (k + 1) * modes]

        for d in range(1, clusters):
            mode_copy(v, d).start()
        own_copy(v).start()

    share = coef_ref.shape[1]
    picked = jnp.zeros((modes, share), jnp.float32)
    for k in range(clusters):
        picked = jnp.where(owner == k, basis[:, k * share : (k + 1) * share], picked)
    coef_ref[...] = picked
    follower = succ_ref[owner]
    mine = jnp.where(label_row == owner, keep, 0.0)
    other = jnp.where(label_row == follower, keep, 0.0).astype(jnp.bfloat16)
    parts = dot(other, jnp.concatenate(pieces, axis=1))
    image = parts[:, 2 * count :] + parts[:, count : 2 * count] + parts[:, :count]
    corr_ref[...] = lax.dot_general(
        mine,
        image,
        (((1,), (1,)), ((), ())),
        precision=lax.Precision.HIGHEST,
        preferred_element_type=jnp.float32,
    )

    @pl.loop(0, variables)
    def _(v):
        for d in range(1, clusters):
            mode_copy(v, d).wait()
        own_copy(v).wait()

    @pl.loop(1, devices)
    def _(d):
        target = lax.rem(me + d, devices)
        when(target < reducers, lambda: part_copy(d)[1].wait_send())
        when(me < reducers, lambda: sum_copy(d).wait_send())


def local(snapshots, labels, start, successor):
    count, variables, width = snapshots.shape
    spaces = lax.axis_size("space")
    clusters = lax.axis_size("clus")
    devices = spaces * clusters
    modes = start.shape[1]
    reducers = min(devices, count // TILE)
    tall = count // reducers
    share = count // clusters
    vmem = pl.BlockSpec(memory_space=pltpu.VMEM)
    hbm = pl.BlockSpec(memory_space=pl.ANY)
    dma = pltpu.SemaphoreType.DMA
    modes_out, coef, corr = pl.pallas_call(
        functools.partial(kernel, (spaces, clusters)),
        out_shape=(
            jax.ShapeDtypeStruct((variables, modes, clusters * width), jnp.bfloat16),
            jax.ShapeDtypeStruct((modes, share), jnp.float32),
            jax.ShapeDtypeStruct((modes, modes), jnp.float32),
        ),
        in_specs=[hbm, vmem, vmem, pl.BlockSpec(memory_space=pltpu.SMEM)],
        out_specs=(hbm, vmem, vmem),
        scratch_shapes=[
            pltpu.VMEM((variables, count, width), jnp.bfloat16),
            pltpu.VMEM((count, count), jnp.float32),
            pltpu.VMEM((devices, tall, count), jnp.float32),
            pltpu.VMEM((tall, count), jnp.float32),
            pltpu.VMEM((count, count), jnp.float32),
            pltpu.VMEM((clusters, variables, modes, width), jnp.bfloat16),
            dma((variables,)),
            dma((devices,)),
            dma((devices,)),
            dma((devices,)),
            dma((devices,)),
            dma((variables, clusters)),
            dma((variables, clusters)),
            dma((variables,)),
        ],
        compiler_params=pltpu.CompilerParams(
            collective_id=0, has_side_effects=True, vmem_limit_bytes=48 * 1024 * 1024
        ),
    )(jnp.transpose(snapshots, (1, 0, 2)), labels.reshape(1, count), start.T, successor)
    return jnp.transpose(modes_out, (1, 0, 2))[None], coef.T, corr[None]


def solution(mesh):
    in_specs = (P("groups", None, ("space", "clus")), P("groups"), P("groups", None), P("groups"))
    out_specs = (
        P(("groups", "clus"), None, None, "space"),
        P(("groups", "clus"), None),
        P(("groups", "clus"), None, None),
    )
    return jax.shard_map(local, mesh=mesh, in_specs=in_specs, out_specs=out_specs, check_vma=False)
```

```python
import functools

import jax
import jax.numpy as jnp
from jax import lax
from jax.experimental import pallas as pl
from jax.experimental.pallas import tpu as pltpu
from jax.sharding import PartitionSpec as P

ITERS = 2
TILE = 8
CAP = 8
CORES = 2
EARLY = 5
VMEM = 64 * 1024 * 1024
MESH = pl.DeviceIdType.MESH


def split3(x):
    high = x.astype(jnp.bfloat16)
    rest = x - high.astype(jnp.float32)
    middle = rest.astype(jnp.bfloat16)
    low = (rest - middle.astype(jnp.float32)).astype(jnp.bfloat16)
    return high, middle, low


def dot(a, b):
    return jnp.dot(a, b, preferred_element_type=jnp.float32)


def times_gram(rows, pieces, count):
    modes = rows.shape[0]
    parts = dot(jnp.concatenate(split3(rows), axis=0), pieces)
    high = parts[:modes]
    middle = parts[modes : 2 * modes, : 2 * count]
    low = parts[2 * modes :, :count]
    return (
        (high[:, 2 * count :] + middle[:, count:] + low)
        + (high[:, count : 2 * count] + middle[:, :count])
        + high[:, :count]
    )


def orthonormal(rows, same):
    modes, count = rows.shape
    half = modes // 2
    first = [0 if j < half else half for j in range(modes)]
    pairs = jnp.concatenate([rows[j : j + 1] * rows[first[j] :] for j in range(modes)], axis=0)
    total = pairs.shape[0]
    sums = dot(jnp.concatenate(split3(pairs), axis=0), same)
    inner = sums[2 * total :] + sums[total : 2 * total] + sums[:total]
    columns = []
    at = 0
    for j in range(modes):
        height = modes - first[j]
        columns.append(inner[at : at + height])
        at += height
    index = lax.broadcasted_iota(jnp.int32, (modes, count), 0)
    result = jnp.zeros_like(rows)
    rest = rows
    for j in range(modes):
        here = j - first[j]
        scale = lax.rsqrt(columns[j][here : here + 1])
        lower = columns[j] * scale
        solved = rest[j - (modes - rest.shape[0]) :][:1] * scale
        result = jnp.where(index == j, solved, result)
        if j == modes - 1:
            break
        if first[j + 1] != first[j]:
            lower = lower[half:]
            rest = rest[half:]
            shift = half
        else:
            shift = first[j]
        rest = rest - lower * solved
        for n in range(j + 1, modes):
            factor = lower[n - shift : n - shift + 1]
            columns[n] = columns[n] - (lower if first[n] == shift else lower[half:]) * factor
    return result


def kernel(
    sizes,
    snap_hbm,
    labels_hbm,
    start_hbm,
    succ_hbm,
    modes_ref,
    coef_ref,
    corr_ref,
    snap,
    labels_ref,
    start_ref,
    succ_ref,
    partial,
    landed,
    chunk,
    gram,
    stage,
    packed,
    got,
    grown,
    load_sem,
    small_sem,
    rs_send,
    rs_recv,
    ag_send,
    ag_recv,
    out_send,
    out_recv,
    early_send,
    early_recv,
    own_sem,
    grown_sem,
):
    spaces, clusters = sizes
    variables, count, width = snap.shape
    modes = start_ref.shape[0]
    devices = spaces * clusters
    reducers = count // TILE if devices > count // TILE else devices
    tall = count // reducers
    units, step = stage.shape[1], stage.shape[3]
    cuts = width // step
    early = packed.shape[1]
    late = units - early
    room = packed.shape[2]
    pairs = clusters // CORES
    owner = lax.axis_index("clus")
    pair, core = owner // CORES, owner % CORES
    me = lax.axis_index("space") * clusters + owner

    def place(index):
        return {"space": index // clusters, "clus": index % clusters}

    def when(condition, body):
        if reducers == devices:
            body()
        else:
            pl.when(condition)(body)

    def load(v):
        return pltpu.make_async_copy(snap_hbm.at[v], snap.at[v], load_sem.at[v])

    small = [
        pltpu.make_async_copy(source, target, small_sem.at[i])
        for i, (source, target) in enumerate(
            ((labels_hbm, labels_ref), (start_hbm, start_ref), (succ_hbm, succ_ref))
        )
    ]
    for v in range(variables):
        load(v).start()
    for copy in small:
        copy.start()
    barrier = pltpu.get_barrier_semaphore()

    @pl.loop(1, devices)
    def _(d):
        target = lax.rem(me + d, devices)
        pl.semaphore_signal(barrier, inc=1, device_id=place(target), device_id_type=MESH)

    partial[...] = jnp.zeros_like(partial)

    @pl.loop(0, variables)
    def _(v):
        load(v).wait()
        block = snap[v]
        partial[...] += lax.dot_general(
            block, block, (((1,), (1,)), ((), ())), preferred_element_type=jnp.float32
        )

    pl.semaphore_wait(barrier, devices - 1)

    def part_copy(d):
        target = lax.rem(me + d, devices)
        rows = pl.ds(pl.multiple_of(target * tall, tall), tall)
        return pltpu.make_async_remote_copy(
            src_ref=partial.at[rows],
            dst_ref=landed.at[d],
            send_sem=rs_send.at[d],
            recv_sem=rs_recv.at[d],
            device_id=place(target),
            device_id_type=MESH,
        )

    def sum_copy(d):
        target = lax.rem(me + d, devices)
        rows = pl.ds(pl.multiple_of(me * tall, tall), tall)
        return pltpu.make_async_remote_copy(
            src_ref=chunk,
            dst_ref=gram.at[rows],
            send_sem=ag_send.at[d],
            recv_sem=ag_recv.at[d],
            device_id=place(target),
            device_id_type=MESH,
        )

    @pl.loop(1, devices)
    def _(d):
        target = lax.rem(me + d, devices)
        when(target < reducers, lambda: part_copy(d).start())

    for copy in small:
        copy.wait()
    label_row = labels_ref[...]
    wide = jnp.broadcast_to(label_row.astype(jnp.float32), (count, count))
    same = (wide == wide.T).astype(jnp.bfloat16)
    before = lax.broadcasted_iota(jnp.int32, (count, count), 0) < lax.broadcasted_iota(
        jnp.int32, (count, count), 1
    )
    rank = dot(
        jnp.ones((16, count), jnp.bfloat16),
        jnp.where(before, same.astype(jnp.float32), 0.0).astype(jnp.bfloat16),
    )[:1].astype(jnp.int32)
    slots = lax.broadcasted_iota(jnp.int32, (room, count), 0)

    def pick(cluster):
        return jnp.where((slots == rank) & (label_row == cluster), 1.0, 0.0)

    def far(hop, c):
        return lax.rem(pair + hop, pairs) * CORES + c

    away = [(hop, c) for hop in range(1, pairs) for c in range(CORES)]

    def early_copy(slot, e):
        hop, c = away[slot]
        return pltpu.make_async_remote_copy(
            src_ref=packed.at[slot, e],
            dst_ref=got.at[(hop - 1) * CORES + core, e],
            send_sem=early_send.at[slot, e],
            recv_sem=early_recv.at[(hop - 1) * CORES + core, e],
            device_id={"clus": far(hop, c)},
            device_id_type=MESH,
        )

    def early_arrival(slot, e):
        return pltpu.make_async_remote_copy(
            src_ref=packed.at[slot, e],
            dst_ref=got.at[slot, e],
            send_sem=early_send.at[slot, e],
            recv_sem=early_recv.at[slot, e],
            device_id={"clus": far(*away[slot])},
            device_id_type=MESH,
        )

    def cells_of(u):
        return u // cuts, pl.ds(pl.multiple_of((u % cuts) * step, step), step)

    def spot(u, source):
        start = pl.multiple_of(source * width + (u % cuts) * step, step)
        return modes_ref.at[u // cuts, :, pl.ds(start, step)]

    picks = jnp.concatenate([pick(far(hop, c)) for hop, c in away], axis=0).astype(jnp.bfloat16)

    def send_early(low, high):
        @pl.loop(low, high)
        def _(e):
            v, cells = cells_of(late + e)
            made = dot(picks, snap[v, :, cells]).astype(jnp.bfloat16)
            for slot in range(len(away)):
                packed[slot, e] = made[slot * room : (slot + 1) * room]
            for slot in range(len(away)):
                early_copy(slot, e).start()

    ahead = early // 2
    send_early(0, ahead)

    def reduce():
        own = pl.ds(pl.multiple_of(me * tall, tall), tall)

        def add(d, total):
            part_copy(d).wait_recv()
            return total + landed[d]

        total = lax.fori_loop(1, devices, add, partial[own])
        total = total * (1.0 / (variables * width * devices))
        chunk[...] = total
        gram[own] = total

        @pl.loop(1, devices)
        def _(d):
            sum_copy(d).start()

    when(me < reducers, reduce)
    send_early(ahead, early)

    @pl.loop(1, devices)
    def _(d):
        source = lax.rem(me + devices - d, devices)
        when(source < reducers, lambda: sum_copy(d).wait_recv())

    pieces = split3(gram[...])
    masked = jnp.concatenate([same * piece for piece in pieces], axis=1)
    basis = start_ref[...]
    for _ in range(ITERS):
        image = times_gram(basis, masked, count) + basis
        basis = orthonormal(image, same)

    keep = basis.astype(jnp.bfloat16).astype(jnp.float32)
    left = jnp.concatenate(
        [jnp.where(label_row == k, keep, 0.0) for k in range(clusters)], axis=0
    ).astype(jnp.bfloat16)

    def mode_copy(u, d):
        target = lax.rem(owner + d, clusters)
        return pltpu.make_async_remote_copy(
            src_ref=stage.at[target, u],
            dst_ref=spot(u, owner),
            send_sem=out_send.at[u, d],
            recv_sem=out_recv.at[u, d],
            device_id={"clus": target},
            device_id_type=MESH,
        )

    def own_copy(u):
        return pltpu.make_async_copy(stage.at[owner, u], spot(u, owner), own_sem.at[u])

    def grown_copy(slot, e):
        source = lax.rem(pair + pairs - away[slot][0], pairs) * CORES + away[slot][1]
        return pltpu.make_async_copy(
            grown.at[slot, e], spot(late + e, source), grown_sem.at[slot, e]
        )

    def make(u):
        v, cells = cells_of(u)
        made = dot(left, snap[v, :, cells]).astype(jnp.bfloat16)
        for k in range(clusters):
            stage[k, u] = made[k * modes : (k + 1) * modes]

    def is_near(d):
        return (owner + d) % clusters // CORES == pair

    @pl.loop(0, late)
    def _(u):
        make(u)
        for d in range(1, clusters):
            mode_copy(u, d).start()
        own_copy(u).start()

    @pl.loop(late, units)
    def _(u):
        make(u)
        for d in range(1, clusters):
            pl.when(is_near(d))(lambda d=d: mode_copy(u, d).start())
        own_copy(u).start()

    share = coef_ref.shape[1]
    picked = jnp.zeros((modes, share), jnp.float32)
    for k in range(clusters):
        picked = jnp.where(owner == k, basis[:, k * share : (k + 1) * share], picked)
    coef_ref[...] = picked
    is_own = lax.broadcasted_iota(jnp.int32, (1, clusters), 1) == owner
    follower = jnp.sum(jnp.where(is_own, succ_ref[...], 0), axis=1, keepdims=True)
    mine = jnp.where(label_row == owner, keep, 0.0)
    other = jnp.where(label_row == follower, keep, 0.0).astype(jnp.bfloat16)
    parts = dot(other, jnp.concatenate(pieces, axis=1))
    image = parts[:, 2 * count :] + parts[:, count : 2 * count] + parts[:, :count]
    corr_ref[...] = lax.dot_general(
        mine,
        image,
        (((1,), (1,)), ((), ())),
        precision=lax.Precision.HIGHEST,
        preferred_element_type=jnp.float32,
    )

    compact = lax.dot_general(
        mine.astype(jnp.bfloat16),
        pick(owner).astype(jnp.bfloat16),
        (((1,), (1,)), ((), ())),
        preferred_element_type=jnp.float32,
    ).astype(jnp.bfloat16)

    @pl.loop(0, early)
    def _(e):
        for slot in range(len(away)):
            early_arrival(slot, e).wait_recv()
            grown[slot, e] = dot(compact, got[slot, e]).astype(jnp.bfloat16)
            grown_copy(slot, e).start()

    @pl.loop(0, late)
    def _(u):
        own_copy(u).wait()
        for d in range(1, clusters):
            mode_copy(u, d).wait()

    @pl.loop(late, units)
    def _(u):
        own_copy(u).wait()
        for d in range(1, clusters):
            pl.when(is_near(d))(lambda d=d: mode_copy(u, d).wait_send())
            pl.when((owner + clusters - d) % clusters // CORES == pair)(
                lambda d=d: mode_copy(u, d).wait_recv()
            )

    @pl.loop(0, early)
    def _(e):
        for slot in range(len(away)):
            early_copy(slot, e).wait_send()
            grown_copy(slot, e).wait()

    @pl.loop(1, devices)
    def _(d):
        target = lax.rem(me + d, devices)
        when(target < reducers, lambda: part_copy(d).wait_send())
        when(me < reducers, lambda: sum_copy(d).wait_send())


def write(*refs):
    half = (len(refs) - 1) // 2
    copies = [
        pltpu.make_async_copy(refs[i], refs[half + i], refs[-1].at[i]) for i in range(half)
    ]
    for copy in copies:
        copy.start()
    for copy in copies:
        copy.wait()


def local(snapshots, labels, start, successor):
    count, variables, width = snapshots.shape
    spaces = lax.axis_size("space")
    clusters = lax.axis_size("clus")
    devices = spaces * clusters
    modes = start.shape[1]
    reducers = min(devices, count // TILE)
    tall = count // reducers
    share = count // clusters
    room = CAP * clusters
    cuts = 3
    units, step = variables * cuts, width // cuts
    away = clusters - CORES
    vmem = pl.BlockSpec(memory_space=pltpu.VMEM)
    hbm = pl.BlockSpec(memory_space=pltpu.HBM)
    dma = pltpu.SemaphoreType.DMA
    results = (
        jax.ShapeDtypeStruct((variables, modes, clusters * width), jnp.bfloat16),
        jax.ShapeDtypeStruct((modes, share), jnp.float32),
        jax.ShapeDtypeStruct((modes, modes), jnp.float32),
    )
    made = pl.pallas_call(
        functools.partial(kernel, (spaces, clusters)),
        out_shape=results,
        in_specs=[hbm] * 4,
        out_specs=(hbm, vmem, vmem),
        scratch_shapes=[
            pltpu.VMEM((variables, count, width), jnp.bfloat16),
            pltpu.VMEM((1, count), jnp.int32),
            pltpu.VMEM((modes, count), jnp.float32),
            pltpu.VMEM((1, clusters), jnp.int32),
            pltpu.VMEM((count, count), jnp.float32),
            pltpu.VMEM((devices, tall, count), jnp.float32),
            pltpu.VMEM((tall, count), jnp.float32),
            pltpu.VMEM((count, count), jnp.float32),
            pltpu.VMEM((clusters, units, modes, step), jnp.bfloat16),
            pltpu.VMEM((away, EARLY, room, step), jnp.bfloat16),
            pltpu.VMEM((away, EARLY, room, step), jnp.bfloat16),
            pltpu.VMEM((away, EARLY, modes, step), jnp.bfloat16),
            dma((variables,)),
            dma((3,)),
            dma((devices,)),
            dma((devices,)),
            dma((devices,)),
            dma((devices,)),
            dma((units, clusters)),
            dma((units, clusters)),
            dma((away, EARLY)),
            dma((away, EARLY)),
            dma((units,)),
            dma((away, EARLY)),
        ],
        compiler_params=pltpu.CompilerParams(
            collective_id=0, has_side_effects=True, vmem_limit_bytes=VMEM
        ),
    )(
        jnp.transpose(snapshots, (1, 0, 2)),
        labels.reshape(1, count),
        start.T,
        successor.reshape(1, clusters),
    )
    modes_out, coef, corr = pl.pallas_call(
        write,
        out_shape=results,
        in_specs=[hbm] * 3,
        out_specs=(hbm,) * 3,
        scratch_shapes=[dma((3,))],
        compiler_params=pltpu.CompilerParams(vmem_limit_bytes=VMEM),
    )(*made)
    return jnp.transpose(modes_out, (1, 0, 2))[None], coef.T, corr[None]


def solution(mesh):
    in_specs = (P("groups", None, ("space", "clus")), P("groups"), P("groups", None), P("groups"))
    out_specs = (
        P(("groups", "clus"), None, None, "space"),
        P(("groups", "clus"), None),
        P(("groups", "clus"), None, None),
    )
    return jax.shard_map(local, mesh=mesh, in_specs=in_specs, out_specs=out_specs, check_vma=False)
```

```python
import functools

import jax
import jax.numpy as jnp
from jax import lax
from jax.experimental import pallas as pl
from jax.experimental.pallas import tpu as pltpu
from jax.sharding import PartitionSpec as P

ITERS = 2
CAP = 8
CORES = 2
EARLY = 4
VMEM = 64 * 1024 * 1024
MESH = pl.DeviceIdType.MESH


def split3(x):
    high = x.astype(jnp.bfloat16)
    rest = x - high.astype(jnp.float32)
    middle = rest.astype(jnp.bfloat16)
    low = (rest - middle.astype(jnp.float32)).astype(jnp.bfloat16)
    return high, middle, low


def dot(a, b):
    return jnp.dot(a, b, preferred_element_type=jnp.float32)


def times_gram(rows, pieces, count):
    modes = rows.shape[0]
    parts = dot(jnp.concatenate(split3(rows), axis=0), pieces)
    high = parts[:modes]
    middle = parts[modes : 2 * modes, : 2 * count]
    low = parts[2 * modes :, :count]
    return (
        (high[:, 2 * count :] + middle[:, count:] + low)
        + (high[:, count : 2 * count] + middle[:, :count])
        + high[:, :count]
    )


def orthonormal(rows, same):
    modes, count = rows.shape
    half = modes // 2
    first = [0 if j < half else half for j in range(modes)]
    pairs = jnp.concatenate([rows[j : j + 1] * rows[first[j] :] for j in range(modes)], axis=0)
    total = pairs.shape[0]
    sums = dot(jnp.concatenate(split3(pairs), axis=0), same)
    inner = sums[2 * total :] + sums[total : 2 * total] + sums[:total]
    columns = []
    at = 0
    for j in range(modes):
        height = modes - first[j]
        columns.append(inner[at : at + height])
        at += height
    index = lax.broadcasted_iota(jnp.int32, (modes, count), 0)
    result = jnp.zeros_like(rows)
    rest = rows
    for j in range(modes):
        here = j - first[j]
        scale = lax.rsqrt(columns[j][here : here + 1])
        lower = columns[j] * scale
        solved = rest[j - (modes - rest.shape[0]) :][:1] * scale
        result = jnp.where(index == j, solved, result)
        if j == modes - 1:
            break
        if first[j + 1] != first[j]:
            lower = lower[half:]
            rest = rest[half:]
            shift = half
        else:
            shift = first[j]
        rest = rest - lower * solved
        for n in range(j + 1, modes):
            factor = lower[n - shift : n - shift + 1]
            columns[n] = columns[n] - (lower if first[n] == shift else lower[half:]) * factor
    return result


def kernel(
    sizes,
    snap_hbm,
    labels_hbm,
    start_hbm,
    succ_hbm,
    modes_ref,
    coef_ref,
    corr_ref,
    snap,
    labels_ref,
    start_ref,
    succ_ref,
    partial,
    crossed,
    summed,
    landed,
    chunk,
    gram,
    stage,
    packed,
    got,
    grown,
    load_sem,
    small_sem,
    cross_send,
    cross_recv,
    rs_send,
    rs_recv,
    ag_send,
    ag_recv,
    out_send,
    out_recv,
    early_send,
    early_recv,
    own_sem,
    grown_sem,
):
    spaces, clusters = sizes
    variables, count, width = snap.shape
    modes = start_ref.shape[0]
    devices = spaces * clusters
    plane = spaces * CORES
    tall = count // plane
    units, step = stage.shape[1], stage.shape[3]
    cuts = width // step
    early = packed.shape[1]
    late = units - early
    room = packed.shape[2]
    pairs = clusters // CORES
    owner = lax.axis_index("clus")
    pair, core = owner // CORES, owner % CORES
    me = lax.axis_index("space") * CORES + core

    def place(index):
        return {"space": index // CORES, "clus": pair * CORES + index % CORES}

    def far(hop, c):
        return lax.rem(pair + hop, pairs) * CORES + c

    away = [(hop, c) for hop in range(1, pairs) for c in range(CORES)]

    def load(v):
        return pltpu.make_async_copy(snap_hbm.at[v], snap.at[v], load_sem.at[v])

    small = [
        pltpu.make_async_copy(source, target, small_sem.at[i])
        for i, (source, target) in enumerate(
            ((labels_hbm, labels_ref), (start_hbm, start_ref), (succ_hbm, succ_ref))
        )
    ]
    for v in range(variables):
        load(v).start()
    for copy in small:
        copy.start()
    barrier = pltpu.get_barrier_semaphore()

    for hop, c in away:
        pl.semaphore_signal(barrier, inc=1, device_id={"clus": far(hop, c)}, device_id_type=MESH)

    @pl.loop(1, plane)
    def _(d):
        target = lax.rem(me + d, plane)
        pl.semaphore_signal(barrier, inc=1, device_id=place(target), device_id_type=MESH)

    partial[...] = jnp.zeros_like(partial)

    @pl.loop(0, variables)
    def _(v):
        load(v).wait()
        block = snap[v]
        partial[...] += lax.dot_general(
            block, block, (((1,), (1,)), ((), ())), preferred_element_type=jnp.float32
        )

    pl.semaphore_wait(barrier, plane - 1 + len(away))

    def cross_copy(hop):
        return pltpu.make_async_remote_copy(
            src_ref=partial,
            dst_ref=crossed.at[hop - 1],
            send_sem=cross_send.at[hop - 1],
            recv_sem=cross_recv.at[hop - 1],
            device_id={"clus": far(hop, core)},
            device_id_type=MESH,
        )

    for hop in range(1, pairs):
        cross_copy(hop).start()

    def part_copy(d):
        target = lax.rem(me + d, plane)
        rows = pl.ds(pl.multiple_of(target * tall, tall), tall)
        return pltpu.make_async_remote_copy(
            src_ref=summed.at[rows],
            dst_ref=landed.at[d],
            send_sem=rs_send.at[d],
            recv_sem=rs_recv.at[d],
            device_id=place(target),
            device_id_type=MESH,
        )

    def sum_copy(d):
        target = lax.rem(me + d, plane)
        rows = pl.ds(pl.multiple_of(me * tall, tall), tall)
        return pltpu.make_async_remote_copy(
            src_ref=chunk,
            dst_ref=gram.at[rows],
            send_sem=ag_send.at[d],
            recv_sem=ag_recv.at[d],
            device_id=place(target),
            device_id_type=MESH,
        )

    for copy in small:
        copy.wait()
    label_row = labels_ref[...]
    wide = jnp.broadcast_to(label_row.astype(jnp.float32), (count, count))
    same = (wide == wide.T).astype(jnp.bfloat16)
    before = lax.broadcasted_iota(jnp.int32, (count, count), 0) < lax.broadcasted_iota(
        jnp.int32, (count, count), 1
    )
    rank = dot(
        jnp.ones((16, count), jnp.bfloat16),
        jnp.where(before, same.astype(jnp.float32), 0.0).astype(jnp.bfloat16),
    )[:1].astype(jnp.int32)
    slots = lax.broadcasted_iota(jnp.int32, (room, count), 0)

    def pick(cluster):
        return jnp.where((slots == rank) & (label_row == cluster), 1.0, 0.0)

    def early_copy(slot, e):
        hop, c = away[slot]
        return pltpu.make_async_remote_copy(
            src_ref=packed.at[slot, e],
            dst_ref=got.at[(hop - 1) * CORES + core, e],
            send_sem=early_send.at[slot, e],
            recv_sem=early_recv.at[(hop - 1) * CORES + core, e],
            device_id={"clus": far(hop, c)},
            device_id_type=MESH,
        )

    def early_arrival(slot, e):
        return pltpu.make_async_remote_copy(
            src_ref=packed.at[slot, e],
            dst_ref=got.at[slot, e],
            send_sem=early_send.at[slot, e],
            recv_sem=early_recv.at[slot, e],
            device_id={"clus": far(*away[slot])},
            device_id_type=MESH,
        )

    def cells_of(u):
        return u // cuts, pl.ds(pl.multiple_of((u % cuts) * step, step), step)

    def spot(u, source):
        start = pl.multiple_of(source * width + (u % cuts) * step, step)
        return modes_ref.at[u // cuts, :, pl.ds(start, step)]

    picks = jnp.concatenate([pick(far(hop, c)) for hop, c in away], axis=0).astype(jnp.bfloat16)

    def send_early(low, high):
        @pl.loop(low, high)
        def _(e):
            v, cells = cells_of(late + e)
            made = dot(picks, snap[v, :, cells]).astype(jnp.bfloat16)
            for slot in range(len(away)):
                packed[slot, e] = made[slot * room : (slot + 1) * room]
            for slot in range(len(away)):
                early_copy(slot, e).start()

    ahead = (early + 1) // 2
    send_early(0, ahead)

    for hop in range(1, pairs):
        cross_copy(hop).wait_recv()
    total = partial[...]
    for hop in range(1, pairs):
        total = total + crossed[hop - 1]
    summed[...] = total

    @pl.loop(1, plane)
    def _(d):
        part_copy(d).start()

    send_early(ahead, early)

    own = pl.ds(pl.multiple_of(me * tall, tall), tall)

    def add(d, total):
        part_copy(d).wait_recv()
        return total + landed[d]

    total = lax.fori_loop(1, plane, add, summed[own])
    total = total * (1.0 / (variables * width * devices))
    chunk[...] = total
    gram[own] = total

    @pl.loop(1, plane)
    def _(d):
        sum_copy(d).start()

    @pl.loop(1, plane)
    def _(d):
        sum_copy(d).wait_recv()

    pieces = split3(gram[...])
    masked = jnp.concatenate([same * piece for piece in pieces], axis=1)
    basis = start_ref[...]
    for _ in range(ITERS):
        image = times_gram(basis, masked, count) + basis
        basis = orthonormal(image, same)

    keep = basis.astype(jnp.bfloat16).astype(jnp.float32)
    left = jnp.concatenate(
        [jnp.where(label_row == k, keep, 0.0) for k in range(clusters)], axis=0
    ).astype(jnp.bfloat16)

    def mode_copy(u, d):
        target = lax.rem(owner + d, clusters)
        return pltpu.make_async_remote_copy(
            src_ref=stage.at[target, u],
            dst_ref=spot(u, owner),
            send_sem=out_send.at[u, d],
            recv_sem=out_recv.at[u, d],
            device_id={"clus": target},
            device_id_type=MESH,
        )

    def own_copy(u):
        return pltpu.make_async_copy(stage.at[owner, u], spot(u, owner), own_sem.at[u])

    def grown_copy(slot, e):
        source = lax.rem(pair + pairs - away[slot][0], pairs) * CORES + away[slot][1]
        return pltpu.make_async_copy(
            grown.at[slot, e], spot(late + e, source), grown_sem.at[slot, e]
        )

    def make(u):
        v, cells = cells_of(u)
        made = dot(left, snap[v, :, cells]).astype(jnp.bfloat16)
        for k in range(clusters):
            stage[k, u] = made[k * modes : (k + 1) * modes]

    def is_near(d):
        return (owner + d) % clusters // CORES == pair

    @pl.loop(0, late)
    def _(u):
        make(u)
        for d in range(1, clusters):
            mode_copy(u, d).start()
        own_copy(u).start()

    @pl.loop(late, units)
    def _(u):
        make(u)
        for d in range(1, clusters):
            pl.when(is_near(d))(lambda d=d: mode_copy(u, d).start())
        own_copy(u).start()

    share = coef_ref.shape[1]
    picked = jnp.zeros((modes, share), jnp.float32)
    for k in range(clusters):
        picked = jnp.where(owner == k, basis[:, k * share : (k + 1) * share], picked)
    coef_ref[...] = picked
    is_own = lax.broadcasted_iota(jnp.int32, (1, clusters), 1) == owner
    follower = jnp.sum(jnp.where(is_own, succ_ref[...], 0), axis=1, keepdims=True)
    mine = jnp.where(label_row == owner, keep, 0.0)
    other = jnp.where(label_row == follower, keep, 0.0).astype(jnp.bfloat16)
    parts = dot(other, jnp.concatenate(pieces, axis=1))
    image = parts[:, 2 * count :] + parts[:, count : 2 * count] + parts[:, :count]
    corr_ref[...] = lax.dot_general(
        mine,
        image,
        (((1,), (1,)), ((), ())),
        precision=lax.Precision.HIGHEST,
        preferred_element_type=jnp.float32,
    )

    compact = lax.dot_general(
        mine.astype(jnp.bfloat16),
        pick(owner).astype(jnp.bfloat16),
        (((1,), (1,)), ((), ())),
        preferred_element_type=jnp.float32,
    ).astype(jnp.bfloat16)

    @pl.loop(0, early)
    def _(e):
        for slot in range(len(away)):
            early_arrival(slot, e).wait_recv()
            grown[slot, e] = dot(compact, got[slot, e]).astype(jnp.bfloat16)
            grown_copy(slot, e).start()

    @pl.loop(0, late)
    def _(u):
        own_copy(u).wait()
        for d in range(1, clusters):
            mode_copy(u, d).wait()

    @pl.loop(late, units)
    def _(u):
        own_copy(u).wait()
        for d in range(1, clusters):
            pl.when(is_near(d))(lambda d=d: mode_copy(u, d).wait_send())
            pl.when((owner + clusters - d) % clusters // CORES == pair)(
                lambda d=d: mode_copy(u, d).wait_recv()
            )

    @pl.loop(0, early)
    def _(e):
        for slot in range(len(away)):
            early_copy(slot, e).wait_send()
            grown_copy(slot, e).wait()

    for hop in range(1, pairs):
        cross_copy(hop).wait_send()

    @pl.loop(1, plane)
    def _(d):
        part_copy(d).wait_send()
        sum_copy(d).wait_send()


def write(*refs):
    half = len(refs) // 2
    for i in range(half):
        refs[half + i][...] = refs[i][...]


def local(snapshots, labels, start, successor):
    count, variables, width = snapshots.shape
    spaces = lax.axis_size("space")
    clusters = lax.axis_size("clus")
    modes = start.shape[1]
    plane = spaces * CORES
    pairs = clusters // CORES
    tall = count // plane
    share = count // clusters
    room = CAP * clusters
    cuts = 3
    units, step = variables * cuts, width // cuts
    away = clusters - CORES
    vmem = pl.BlockSpec(memory_space=pltpu.VMEM)
    hbm = pl.BlockSpec(memory_space=pltpu.HBM)
    dma = pltpu.SemaphoreType.DMA
    results = (
        jax.ShapeDtypeStruct((variables, modes, clusters * width), jnp.bfloat16),
        jax.ShapeDtypeStruct((modes, share), jnp.float32),
        jax.ShapeDtypeStruct((modes, modes), jnp.float32),
    )
    made = pl.pallas_call(
        functools.partial(kernel, (spaces, clusters)),
        out_shape=results,
        in_specs=[hbm] * 4,
        out_specs=(hbm, vmem, vmem),
        scratch_shapes=[
            pltpu.VMEM((variables, count, width), jnp.bfloat16),
            pltpu.VMEM((1, count), jnp.int32),
            pltpu.VMEM((modes, count), jnp.float32),
            pltpu.VMEM((1, clusters), jnp.int32),
            pltpu.VMEM((count, count), jnp.float32),
            pltpu.VMEM((pairs - 1, count, count), jnp.float32),
            pltpu.VMEM((count, count), jnp.float32),
            pltpu.VMEM((plane, tall, count), jnp.float32),
            pltpu.VMEM((tall, count), jnp.float32),
            pltpu.VMEM((count, count), jnp.float32),
            pltpu.VMEM((clusters, units, modes, step), jnp.bfloat16),
            pltpu.VMEM((away, EARLY, room, step), jnp.bfloat16),
            pltpu.VMEM((away, EARLY, room, step), jnp.bfloat16),
            pltpu.VMEM((away, EARLY, modes, step), jnp.bfloat16),
            dma((variables,)),
            dma((3,)),
            dma((pairs - 1,)),
            dma((pairs - 1,)),
            dma((plane,)),
            dma((plane,)),
            dma((plane,)),
            dma((plane,)),
            dma((units, clusters)),
            dma((units, clusters)),
            dma((away, EARLY)),
            dma((away, EARLY)),
            dma((units,)),
            dma((away, EARLY)),
        ],
        compiler_params=pltpu.CompilerParams(
            collective_id=0, has_side_effects=True, vmem_limit_bytes=VMEM
        ),
    )(
        jnp.transpose(snapshots, (1, 0, 2)),
        labels.reshape(1, count),
        start.T,
        successor.reshape(1, clusters),
    )
    blocks = [
        pl.BlockSpec((1, modes, clusters * width), lambda v: (v, 0, 0)),
        pl.BlockSpec((modes, share), lambda v: (0, 0)),
        pl.BlockSpec((modes, modes), lambda v: (0, 0)),
    ]
    modes_out, coef, corr = pl.pallas_call(
        write,
        grid=(variables,),
        out_shape=results,
        in_specs=blocks,
        out_specs=blocks,
        compiler_params=pltpu.CompilerParams(vmem_limit_bytes=VMEM),
    )(*made)
    return jnp.transpose(modes_out, (1, 0, 2))[None], coef.T, corr[None]


def solution(mesh):
    in_specs = (P("groups", None, ("space", "clus")), P("groups"), P("groups", None), P("groups"))
    out_specs = (
        P(("groups", "clus"), None, None, "space"),
        P(("groups", "clus"), None),
        P(("groups", "clus"), None, None),
    )
    return jax.shard_map(local, mesh=mesh, in_specs=in_specs, out_specs=out_specs, check_vma=False)
```

```python
import functools

import jax
import jax.numpy as jnp
from jax import lax
from jax.experimental import pallas as pl
from jax.experimental.pallas import tpu as pltpu
from jax.sharding import PartitionSpec as P

ITERS = 2
CAP = 8
CORES = 2
EARLY = 5
VMEM = 64 * 1024 * 1024
MESH = pl.DeviceIdType.MESH


def split3(x):
    high = x.astype(jnp.bfloat16)
    rest = x - high.astype(jnp.float32)
    middle = rest.astype(jnp.bfloat16)
    low = (rest - middle.astype(jnp.float32)).astype(jnp.bfloat16)
    return high, middle, low


def dot(a, b):
    return jnp.dot(a, b, preferred_element_type=jnp.float32)


def times_gram(rows, pieces, count):
    modes = rows.shape[0]
    parts = dot(jnp.concatenate(split3(rows), axis=0), pieces)
    high = parts[:modes]
    middle = parts[modes : 2 * modes, : 2 * count]
    low = parts[2 * modes :, :count]
    return (
        (high[:, 2 * count :] + middle[:, count:] + low)
        + (high[:, count : 2 * count] + middle[:, :count])
        + high[:, :count]
    )


def orthonormal(rows, same):
    modes, count = rows.shape
    half = modes // 2
    first = [0 if j < half else half for j in range(modes)]
    pairs = jnp.concatenate([rows[j : j + 1] * rows[first[j] :] for j in range(modes)], axis=0)
    total = pairs.shape[0]
    sums = dot(jnp.concatenate(split3(pairs), axis=0), same)
    inner = sums[2 * total :] + sums[total : 2 * total] + sums[:total]
    columns = []
    at = 0
    for j in range(modes):
        height = modes - first[j]
        columns.append(inner[at : at + height])
        at += height
    index = lax.broadcasted_iota(jnp.int32, (modes, count), 0)
    result = jnp.zeros_like(rows)
    rest = rows
    for j in range(modes):
        here = j - first[j]
        scale = lax.rsqrt(columns[j][here : here + 1])
        lower = columns[j] * scale
        solved = rest[j - (modes - rest.shape[0]) :][:1] * scale
        result = jnp.where(index == j, solved, result)
        if j == modes - 1:
            break
        if first[j + 1] != first[j]:
            lower = lower[half:]
            rest = rest[half:]
            shift = half
        else:
            shift = first[j]
        rest = rest - lower * solved
        for n in range(j + 1, modes):
            factor = lower[n - shift : n - shift + 1]
            columns[n] = columns[n] - (lower if first[n] == shift else lower[half:]) * factor
    return result


def kernel(
    sizes,
    snap_hbm,
    labels_hbm,
    start_hbm,
    succ_hbm,
    modes_ref,
    coef_ref,
    corr_ref,
    snap,
    labels_ref,
    start_ref,
    succ_ref,
    partial,
    crossed,
    summed,
    landed,
    chunk,
    gram,
    stage,
    packed,
    got,
    grown,
    load_sem,
    small_sem,
    cross_send,
    cross_recv,
    rs_send,
    rs_recv,
    ag_send,
    ag_recv,
    out_send,
    out_recv,
    early_send,
    early_recv,
    own_sem,
    grown_sem,
):
    spaces, clusters = sizes
    variables, count, width = snap.shape
    modes = start_ref.shape[0]
    devices = spaces * clusters
    plane = spaces * CORES
    tall = count // plane
    units, step = stage.shape[1], stage.shape[3]
    cuts = width // step
    early = packed.shape[1]
    late = units - early
    room = packed.shape[2]
    pairs = clusters // CORES
    owner = lax.axis_index("clus")
    pair, core = owner // CORES, owner % CORES
    me = lax.axis_index("space") * CORES + core

    def place(index):
        return {"space": index // CORES, "clus": pair * CORES + index % CORES}

    def far(hop, c):
        return lax.rem(pair + hop, pairs) * CORES + c

    away = [(hop, c) for hop in range(1, pairs) for c in range(CORES)]

    def load(v):
        return pltpu.make_async_copy(snap_hbm.at[v], snap.at[v], load_sem.at[v])

    small = [
        pltpu.make_async_copy(source, target, small_sem.at[i])
        for i, (source, target) in enumerate(
            ((labels_hbm, labels_ref), (start_hbm, start_ref), (succ_hbm, succ_ref))
        )
    ]
    for copy in small:
        copy.start()
    for v in (variables - 1, *range(variables - 1)):
        load(v).start()
    barrier = pltpu.get_barrier_semaphore()

    for hop, c in away:
        pl.semaphore_signal(barrier, inc=1, device_id={"clus": far(hop, c)}, device_id_type=MESH)

    @pl.loop(1, plane)
    def _(d):
        target = lax.rem(me + d, plane)
        pl.semaphore_signal(barrier, inc=1, device_id=place(target), device_id_type=MESH)

    for copy in small:
        copy.wait()
    label_row = labels_ref[...]
    wide = jnp.broadcast_to(label_row.astype(jnp.float32), (count, count))
    same = (wide == wide.T).astype(jnp.bfloat16)
    before = lax.broadcasted_iota(jnp.int32, (count, count), 0) < lax.broadcasted_iota(
        jnp.int32, (count, count), 1
    )
    rank = dot(
        jnp.ones((16, count), jnp.bfloat16),
        jnp.where(before, same.astype(jnp.float32), 0.0).astype(jnp.bfloat16),
    )[:1].astype(jnp.int32)
    slots = lax.broadcasted_iota(jnp.int32, (room, count), 0)

    def pick(cluster):
        return jnp.where((slots == rank) & (label_row == cluster), 1.0, 0.0)

    def early_copy(slot, e):
        hop, c = away[slot]
        return pltpu.make_async_remote_copy(
            src_ref=packed.at[slot, e],
            dst_ref=got.at[(hop - 1) * CORES + core, e],
            send_sem=early_send.at[slot, e],
            recv_sem=early_recv.at[(hop - 1) * CORES + core, e],
            device_id={"clus": far(hop, c)},
            device_id_type=MESH,
        )

    def early_arrival(slot, e):
        return pltpu.make_async_remote_copy(
            src_ref=packed.at[slot, e],
            dst_ref=got.at[slot, e],
            send_sem=early_send.at[slot, e],
            recv_sem=early_recv.at[slot, e],
            device_id={"clus": far(*away[slot])},
            device_id_type=MESH,
        )

    def cells_of(u):
        return u // cuts, pl.ds(pl.multiple_of((u % cuts) * step, step), step)

    def spot(u, source):
        start = pl.multiple_of(source * width + (u % cuts) * step, step)
        return modes_ref.at[u // cuts, :, pl.ds(start, step)]

    picks = jnp.concatenate([pick(far(hop, c)) for hop, c in away], axis=0).astype(jnp.bfloat16)

    def send_early(low, high):
        @pl.loop(low, high)
        def _(e):
            v, cells = cells_of(late + e)
            made = dot(picks, snap[v, :, cells]).astype(jnp.bfloat16)
            for slot in range(len(away)):
                packed[slot, e] = made[slot * room : (slot + 1) * room]
            for slot in range(len(away)):
                early_copy(slot, e).start()

    load(variables - 1).wait()
    pl.semaphore_wait(barrier, plane - 1 + len(away))
    send_early(early - 1, early)

    partial[...] = jnp.zeros_like(partial)

    @pl.loop(0, variables)
    def _(turn):
        v = lax.rem(turn + variables - 1, variables)
        pl.when(turn > 0)(lambda: load(v).wait())
        block = snap[v]
        partial[...] += lax.dot_general(
            block, block, (((1,), (1,)), ((), ())), preferred_element_type=jnp.float32
        )

    def cross_copy(hop):
        return pltpu.make_async_remote_copy(
            src_ref=partial,
            dst_ref=crossed.at[hop - 1],
            send_sem=cross_send.at[hop - 1],
            recv_sem=cross_recv.at[hop - 1],
            device_id={"clus": far(hop, core)},
            device_id_type=MESH,
        )

    for hop in range(1, pairs):
        cross_copy(hop).start()

    def part_copy(d):
        target = lax.rem(me + d, plane)
        rows = pl.ds(pl.multiple_of(target * tall, tall), tall)
        return pltpu.make_async_remote_copy(
            src_ref=summed.at[rows],
            dst_ref=landed.at[d],
            send_sem=rs_send.at[d],
            recv_sem=rs_recv.at[d],
            device_id=place(target),
            device_id_type=MESH,
        )

    def sum_copy(d):
        target = lax.rem(me + d, plane)
        rows = pl.ds(pl.multiple_of(me * tall, tall), tall)
        return pltpu.make_async_remote_copy(
            src_ref=chunk,
            dst_ref=gram.at[rows],
            send_sem=ag_send.at[d],
            recv_sem=ag_recv.at[d],
            device_id=place(target),
            device_id_type=MESH,
        )

    ahead = early // 2
    send_early(0, ahead)

    for hop in range(1, pairs):
        cross_copy(hop).wait_recv()
    total = partial[...]
    for hop in range(1, pairs):
        total = total + crossed[hop - 1]
    summed[...] = total

    @pl.loop(1, plane)
    def _(d):
        part_copy(d).start()

    send_early(ahead, early - 1)

    own = pl.ds(pl.multiple_of(me * tall, tall), tall)

    def add(d, total):
        part_copy(d).wait_recv()
        return total + landed[d]

    total = lax.fori_loop(1, plane, add, summed[own])
    total = total * (1.0 / (variables * width * devices))
    chunk[...] = total
    gram[own] = total

    @pl.loop(1, plane)
    def _(d):
        sum_copy(d).start()

    @pl.loop(1, plane)
    def _(d):
        sum_copy(d).wait_recv()

    pieces = split3(gram[...])
    masked = jnp.concatenate([same * piece for piece in pieces], axis=1)
    basis = start_ref[...]
    for _ in range(ITERS):
        image = times_gram(basis, masked, count) + basis
        basis = orthonormal(image, same)

    keep = basis.astype(jnp.bfloat16).astype(jnp.float32)
    left = jnp.concatenate(
        [jnp.where(label_row == k, keep, 0.0) for k in range(clusters)], axis=0
    ).astype(jnp.bfloat16)

    def mode_copy(u, d):
        target = lax.rem(owner + d, clusters)
        return pltpu.make_async_remote_copy(
            src_ref=stage.at[target, u],
            dst_ref=spot(u, owner),
            send_sem=out_send.at[u, d],
            recv_sem=out_recv.at[u, d],
            device_id={"clus": target},
            device_id_type=MESH,
        )

    def own_copy(u):
        return pltpu.make_async_copy(stage.at[owner, u], spot(u, owner), own_sem.at[u])

    def grown_copy(slot, e):
        source = lax.rem(pair + pairs - away[slot][0], pairs) * CORES + away[slot][1]
        return pltpu.make_async_copy(
            grown.at[slot, e], spot(late + e, source), grown_sem.at[slot, e]
        )

    def make(u):
        v, cells = cells_of(u)
        made = dot(left, snap[v, :, cells]).astype(jnp.bfloat16)
        for k in range(clusters):
            stage[k, u] = made[k * modes : (k + 1) * modes]

    def is_near(d):
        return (owner + d) % clusters // CORES == pair

    @pl.loop(0, late)
    def _(u):
        make(u)
        for d in range(1, clusters):
            mode_copy(u, d).start()
        own_copy(u).start()

    @pl.loop(late, units)
    def _(u):
        make(u)
        for d in range(1, clusters):
            pl.when(is_near(d))(lambda d=d: mode_copy(u, d).start())
        own_copy(u).start()

    share = coef_ref.shape[1]
    picked = jnp.zeros((modes, share), jnp.float32)
    for k in range(clusters):
        picked = jnp.where(owner == k, basis[:, k * share : (k + 1) * share], picked)
    coef_ref[...] = picked
    is_own = lax.broadcasted_iota(jnp.int32, (1, clusters), 1) == owner
    follower = jnp.sum(jnp.where(is_own, succ_ref[...], 0), axis=1, keepdims=True)
    mine = jnp.where(label_row == owner, keep, 0.0)
    other = jnp.where(label_row == follower, keep, 0.0).astype(jnp.bfloat16)
    parts = dot(other, jnp.concatenate(pieces, axis=1))
    image = parts[:, 2 * count :] + parts[:, count : 2 * count] + parts[:, :count]
    corr_ref[...] = lax.dot_general(
        mine,
        image,
        (((1,), (1,)), ((), ())),
        precision=lax.Precision.HIGHEST,
        preferred_element_type=jnp.float32,
    )

    compact = lax.dot_general(
        mine.astype(jnp.bfloat16),
        pick(owner).astype(jnp.bfloat16),
        (((1,), (1,)), ((), ())),
        preferred_element_type=jnp.float32,
    ).astype(jnp.bfloat16)

    @pl.loop(0, early)
    def _(e):
        for slot in range(len(away)):
            early_arrival(slot, e).wait_recv()
            grown[slot, e] = dot(compact, got[slot, e]).astype(jnp.bfloat16)
            grown_copy(slot, e).start()

    for hop in range(1, pairs):
        cross_copy(hop).wait_send()

    @pl.loop(1, plane)
    def _(d):
        part_copy(d).wait_send()
        sum_copy(d).wait_send()

    @pl.loop(0, early)
    def _(e):
        for slot in range(len(away)):
            early_copy(slot, e).wait_send()
            grown_copy(slot, e).wait()

    @pl.loop(late, units)
    def _(u):
        own_copy(u).wait()
        for d in range(1, clusters):
            pl.when(is_near(d))(lambda d=d: mode_copy(u, d).wait_send())
            pl.when((owner + clusters - d) % clusters // CORES == pair)(
                lambda d=d: mode_copy(u, d).wait_recv()
            )

    @pl.loop(0, late)
    def _(u):
        own_copy(u).wait()
        for d in range(1, clusters):
            mode_copy(u, d).wait()


def write(*refs):
    inputs, outputs, held, read_sem, write_sem = refs[:3], refs[3:6], refs[6:9], *refs[9:]
    variables = inputs[0].shape[0]
    parts = [(0, v) for v in range(variables)] + [(1, None), (2, None)]

    def piece(arrays, part):
        ref = arrays[part[0]]
        return ref if part[1] is None else ref.at[part[1]]

    reads = [
        pltpu.make_async_copy(piece(inputs, part), piece(held, part), read_sem.at[i])
        for i, part in enumerate(parts)
    ]
    writes = [
        pltpu.make_async_copy(piece(held, part), piece(outputs, part), write_sem.at[i])
        for i, part in enumerate(parts)
    ]
    for copy in reads:
        copy.start()
    for read, copy in zip(reads, writes):
        read.wait()
        copy.start()
    for copy in writes:
        copy.wait()


def local(snapshots, labels, start, successor):
    count, variables, width = snapshots.shape
    spaces = lax.axis_size("space")
    clusters = lax.axis_size("clus")
    modes = start.shape[1]
    plane = spaces * CORES
    pairs = clusters // CORES
    tall = count // plane
    share = count // clusters
    room = CAP * clusters
    cuts = 3
    units, step = variables * cuts, width // cuts
    away = clusters - CORES
    vmem = pl.BlockSpec(memory_space=pltpu.VMEM)
    hbm = pl.BlockSpec(memory_space=pltpu.HBM)
    dma = pltpu.SemaphoreType.DMA
    results = (
        jax.ShapeDtypeStruct((variables, modes, clusters * width), jnp.bfloat16),
        jax.ShapeDtypeStruct((modes, share), jnp.float32),
        jax.ShapeDtypeStruct((modes, modes), jnp.float32),
    )
    made = pl.pallas_call(
        functools.partial(kernel, (spaces, clusters)),
        out_shape=results,
        in_specs=[hbm] * 4,
        out_specs=(hbm, vmem, vmem),
        scratch_shapes=[
            pltpu.VMEM((variables, count, width), jnp.bfloat16),
            pltpu.VMEM((1, count), jnp.int32),
            pltpu.VMEM((modes, count), jnp.float32),
            pltpu.VMEM((1, clusters), jnp.int32),
            pltpu.VMEM((count, count), jnp.float32),
            pltpu.VMEM((pairs - 1, count, count), jnp.float32),
            pltpu.VMEM((count, count), jnp.float32),
            pltpu.VMEM((plane, tall, count), jnp.float32),
            pltpu.VMEM((tall, count), jnp.float32),
            pltpu.VMEM((count, count), jnp.float32),
            pltpu.VMEM((clusters, units, modes, step), jnp.bfloat16),
            pltpu.VMEM((away, EARLY, room, step), jnp.bfloat16),
            pltpu.VMEM((away, EARLY, room, step), jnp.bfloat16),
            pltpu.VMEM((away, EARLY, modes, step), jnp.bfloat16),
            dma((variables,)),
            dma((3,)),
            dma((pairs - 1,)),
            dma((pairs - 1,)),
            dma((plane,)),
            dma((plane,)),
            dma((plane,)),
            dma((plane,)),
            dma((units, clusters)),
            dma((units, clusters)),
            dma((away, EARLY)),
            dma((away, EARLY)),
            dma((units,)),
            dma((away, EARLY)),
        ],
        compiler_params=pltpu.CompilerParams(
            collective_id=0, has_side_effects=True, vmem_limit_bytes=VMEM
        ),
    )(
        jnp.transpose(snapshots, (1, 0, 2)),
        labels.reshape(1, count),
        start.T,
        successor.reshape(1, clusters),
    )
    modes_out, coef, corr = pl.pallas_call(
        write,
        out_shape=results,
        in_specs=[hbm] * 3,
        out_specs=(hbm,) * 3,
        scratch_shapes=[pltpu.VMEM(x.shape, x.dtype) for x in results]
        + [dma((variables + 2,)), dma((variables + 2,))],
        compiler_params=pltpu.CompilerParams(vmem_limit_bytes=VMEM),
    )(*made)
    return jnp.transpose(modes_out, (1, 0, 2))[None], coef.T, corr[None]


def solution(mesh):
    in_specs = (P("groups", None, ("space", "clus")), P("groups"), P("groups", None), P("groups"))
    out_specs = (
        P(("groups", "clus"), None, None, "space"),
        P(("groups", "clus"), None),
        P(("groups", "clus"), None, None),
    )
    return jax.shard_map(local, mesh=mesh, in_specs=in_specs, out_specs=out_specs, check_vma=False)
```

```python
import functools

import jax
import jax.numpy as jnp
from jax import lax
from jax.experimental import pallas as pl
from jax.experimental.pallas import tpu as pltpu
from jax.sharding import PartitionSpec as P

ITERS = 2
CAP = 8
CORES = 2
EARLY = 6
VMEM = 64 * 1024 * 1024
MESH = pl.DeviceIdType.MESH


def split3(x):
    high = x.astype(jnp.bfloat16)
    rest = x - high.astype(jnp.float32)
    middle = rest.astype(jnp.bfloat16)
    low = (rest - middle.astype(jnp.float32)).astype(jnp.bfloat16)
    return high, middle, low


def dot(a, b):
    return jnp.dot(a, b, preferred_element_type=jnp.float32)


def times_gram(rows, pieces, count):
    modes = rows.shape[0]
    parts = dot(jnp.concatenate(split3(rows), axis=0), pieces)
    high = parts[:modes]
    middle = parts[modes : 2 * modes, : 2 * count]
    low = parts[2 * modes :, :count]
    return (
        (high[:, 2 * count :] + middle[:, count:] + low)
        + (high[:, count : 2 * count] + middle[:, :count])
        + high[:, :count]
    )


def orthonormal(rows, same):
    modes, count = rows.shape
    half = modes // 2
    first = [0 if j < half else half for j in range(modes)]
    pairs = jnp.concatenate([rows[j : j + 1] * rows[first[j] :] for j in range(modes)], axis=0)
    total = pairs.shape[0]
    sums = dot(jnp.concatenate(split3(pairs), axis=0), same)
    inner = sums[2 * total :] + sums[total : 2 * total] + sums[:total]
    columns = []
    at = 0
    for j in range(modes):
        height = modes - first[j]
        columns.append(inner[at : at + height])
        at += height
    index = lax.broadcasted_iota(jnp.int32, (modes, count), 0)
    result = jnp.zeros_like(rows)
    rest = rows
    for j in range(modes):
        here = j - first[j]
        scale = lax.rsqrt(columns[j][here : here + 1])
        lower = columns[j] * scale
        solved = rest[j - (modes - rest.shape[0]) :][:1] * scale
        result = jnp.where(index == j, solved, result)
        if j == modes - 1:
            break
        if first[j + 1] != first[j]:
            lower = lower[half:]
            rest = rest[half:]
            shift = half
        else:
            shift = first[j]
        rest = rest - lower * solved
        for n in range(j + 1, modes):
            factor = lower[n - shift : n - shift + 1]
            columns[n] = columns[n] - (lower if first[n] == shift else lower[half:]) * factor
    return result


def kernel(
    sizes,
    snap_hbm,
    labels_hbm,
    start_hbm,
    succ_hbm,
    modes_ref,
    coef_ref,
    corr_ref,
    snap,
    labels_ref,
    start_ref,
    succ_ref,
    partial,
    crossed,
    summed,
    landed,
    chunk,
    gram,
    stage,
    packed,
    got,
    grown,
    load_sem,
    small_sem,
    cross_send,
    cross_recv,
    rs_send,
    rs_recv,
    ag_send,
    ag_recv,
    out_send,
    out_recv,
    early_send,
    early_recv,
    own_sem,
    grown_sem,
):
    spaces, clusters = sizes
    variables, count, width = snap.shape
    modes = start_ref.shape[0]
    devices = spaces * clusters
    plane = spaces * CORES
    tall = count // plane
    units, step = stage.shape[1], stage.shape[3]
    cuts = width // step
    early = packed.shape[1]
    late = units - early
    room = packed.shape[2]
    pairs = clusters // CORES
    owner = lax.axis_index("clus")
    pair, core = owner // CORES, owner % CORES
    space = lax.axis_index("space")
    me = space * CORES + core
    near = pair * CORES + 1 - core
    steps = [(ds, dc) for ds in range(spaces) for dc in range(CORES) if ds + dc]

    def place(d):
        ds, dc = steps[d]
        return lax.rem(space + ds, spaces), 1 - core if dc else core

    def device(d):
        z, c = place(d)
        return {"space": z, "clus": pair * CORES + c}

    def far(hop, c):
        return lax.rem(pair + hop, pairs) * CORES + c

    away = [(hop, c) for hop in range(1, pairs) for c in range(CORES)]

    def load(v):
        return pltpu.make_async_copy(snap_hbm.at[v], snap.at[v], load_sem.at[v])

    small = [
        pltpu.make_async_copy(source, target, small_sem.at[i])
        for i, (source, target) in enumerate(
            ((labels_hbm, labels_ref), (start_hbm, start_ref), (succ_hbm, succ_ref))
        )
    ]
    for copy in small:
        copy.start()
    for v in (variables - 1, *range(variables - 1)):
        load(v).start()
    barrier = pltpu.get_barrier_semaphore()

    for hop, c in away:
        pl.semaphore_signal(barrier, inc=1, device_id={"clus": far(hop, c)}, device_id_type=MESH)

    for d in range(len(steps)):
        pl.semaphore_signal(barrier, inc=1, device_id=device(d), device_id_type=MESH)

    for copy in small:
        copy.wait()
    label_row = labels_ref[...]
    wide = jnp.broadcast_to(label_row.astype(jnp.float32), (count, count))
    same = (wide == wide.T).astype(jnp.bfloat16)
    before = lax.broadcasted_iota(jnp.int32, (count, count), 0) < lax.broadcasted_iota(
        jnp.int32, (count, count), 1
    )
    rank = dot(
        jnp.ones((16, count), jnp.bfloat16),
        jnp.where(before, same.astype(jnp.float32), 0.0).astype(jnp.bfloat16),
    )[:1].astype(jnp.int32)
    slots = lax.broadcasted_iota(jnp.int32, (room, count), 0)

    def pick(cluster):
        return jnp.where((slots == rank) & (label_row == cluster), 1.0, 0.0)

    def early_copy(slot, e):
        hop, c = away[slot]
        return pltpu.make_async_remote_copy(
            src_ref=packed.at[slot, e],
            dst_ref=got.at[(hop - 1) * CORES + core, e],
            send_sem=early_send.at[slot, e],
            recv_sem=early_recv.at[(hop - 1) * CORES + core, e],
            device_id={"clus": far(hop, c)},
            device_id_type=MESH,
        )

    def early_arrival(slot, e):
        return pltpu.make_async_remote_copy(
            src_ref=packed.at[slot, e],
            dst_ref=got.at[slot, e],
            send_sem=early_send.at[slot, e],
            recv_sem=early_recv.at[slot, e],
            device_id={"clus": far(*away[slot])},
            device_id_type=MESH,
        )

    def cells_of(u):
        return u // cuts, pl.ds(pl.multiple_of((u % cuts) * step, step), step)

    def spot(u, source):
        start = pl.multiple_of(source * width + (u % cuts) * step, step)
        return modes_ref.at[u // cuts, :, pl.ds(start, step)]

    picks = jnp.concatenate([pick(far(hop, c)) for hop, c in away], axis=0).astype(jnp.bfloat16)

    def send_early(low, high):
        @pl.loop(low, high)
        def _(e):
            v, cells = cells_of(late + e)
            made = dot(picks, snap[v, :, cells]).astype(jnp.bfloat16)
            for slot in range(len(away)):
                packed[slot, e] = made[slot * room : (slot + 1) * room]
            for slot in range(len(away)):
                early_copy(slot, e).start()

    partial[...] = jnp.zeros_like(partial)

    def add_gram(low, high):
        @pl.loop(low, high)
        def _(turn):
            v = lax.rem(turn + variables - 1, variables)
            load(v).wait()
            block = snap[v]
            partial[...] += lax.dot_general(
                block, block, (((1,), (1,)), ((), ())), preferred_element_type=jnp.float32
            )

    def part_copy(d):
        z, c = place(d)
        rows = pl.ds(pl.multiple_of((z * CORES + c) * tall, tall), tall)
        return pltpu.make_async_remote_copy(
            src_ref=partial.at[rows],
            dst_ref=landed.at[d],
            send_sem=rs_send.at[d],
            recv_sem=rs_recv.at[d],
            device_id=device(d),
            device_id_type=MESH,
        )

    def cross_copy(hop):
        return pltpu.make_async_remote_copy(
            src_ref=chunk,
            dst_ref=crossed.at[hop - 1],
            send_sem=cross_send.at[hop - 1],
            recv_sem=cross_recv.at[hop - 1],
            device_id={"clus": far(hop, core)},
            device_id_type=MESH,
        )

    own = pl.ds(pl.multiple_of(me * tall, tall), tall)

    def sum_copy(d):
        return pltpu.make_async_remote_copy(
            src_ref=summed,
            dst_ref=gram.at[own],
            send_sem=ag_send.at[d],
            recv_sem=ag_recv.at[d],
            device_id=device(d),
            device_id_type=MESH,
        )

    others = range(len(steps))
    first = variables - 2
    add_gram(0, first)
    pl.semaphore_wait(barrier, len(steps) + len(away))
    send_early(early - 1, early)
    add_gram(first, variables)
    for d in others:
        part_copy(d).start()
    send_early(0, 1)

    total = partial[own]
    for d in others:
        part_copy(d).wait_recv()
        total = total + landed[d]
    chunk[...] = total
    for hop in range(1, pairs):
        cross_copy(hop).start()
    send_early(1, 3)
    for hop in range(1, pairs):
        cross_copy(hop).wait_recv()
        total = total + crossed[hop - 1]
    total = total * (1.0 / (variables * width * devices))
    summed[...] = total
    gram[own] = total
    for d in others:
        sum_copy(d).start()
    send_early(3, early - 1)
    for d in others:
        sum_copy(d).wait_recv()

    pieces = split3(gram[...])
    masked = jnp.concatenate([same * piece for piece in pieces], axis=1)
    basis = start_ref[...]
    for _ in range(ITERS):
        image = times_gram(basis, masked, count) + basis
        basis = orthonormal(image, same)

    keep = basis.astype(jnp.bfloat16).astype(jnp.float32)
    left = jnp.concatenate(
        [jnp.where(label_row == k, keep, 0.0) for k in range(clusters)], axis=0
    ).astype(jnp.bfloat16)

    def mode_copy(u, target, slot_out, slot_in):
        return pltpu.make_async_remote_copy(
            src_ref=stage.at[target, u],
            dst_ref=spot(u, owner),
            send_sem=out_send.at[u, slot_out],
            recv_sem=out_recv.at[u, slot_in],
            device_id={"clus": target},
            device_id_type=MESH,
        )

    def near_copy(u):
        return mode_copy(u, near, 0, 0)

    def far_copy(u, slot):
        hop, c = away[slot]
        return mode_copy(u, far(hop, c), 1 + slot, 1 + (hop - 1) * CORES + core)

    def far_arrival(u, slot):
        return mode_copy(u, far(*away[slot]), 1 + slot, 1 + slot)

    def own_copy(u):
        return pltpu.make_async_copy(stage.at[owner, u], spot(u, owner), own_sem.at[u])

    def grown_copy(slot, e):
        source = lax.rem(pair + pairs - away[slot][0], pairs) * CORES + away[slot][1]
        return pltpu.make_async_copy(
            grown.at[slot, e], spot(late + e, source), grown_sem.at[slot, e]
        )

    def make(u):
        v, cells = cells_of(u)
        made = dot(left, snap[v, :, cells]).astype(jnp.bfloat16)
        for k in range(clusters):
            stage[k, u] = made[k * modes : (k + 1) * modes]

    @pl.loop(0, late)
    def _(u):
        make(u)
        for slot in range(len(away)):
            far_copy(u, slot).start()
        near_copy(u).start()
        own_copy(u).start()

    @pl.loop(late, units)
    def _(u):
        make(u)
        near_copy(u).start()
        own_copy(u).start()

    share = coef_ref.shape[1]
    picked = jnp.zeros((modes, share), jnp.float32)
    for k in range(clusters):
        picked = jnp.where(owner == k, basis[:, k * share : (k + 1) * share], picked)
    coef_ref[...] = picked
    is_own = lax.broadcasted_iota(jnp.int32, (1, clusters), 1) == owner
    follower = jnp.sum(jnp.where(is_own, succ_ref[...], 0), axis=1, keepdims=True)
    mine = jnp.where(label_row == owner, keep, 0.0)
    other = jnp.where(label_row == follower, keep, 0.0).astype(jnp.bfloat16)
    parts = dot(other, jnp.concatenate(pieces, axis=1))
    image = parts[:, 2 * count :] + parts[:, count : 2 * count] + parts[:, :count]
    corr_ref[...] = lax.dot_general(
        mine,
        image,
        (((1,), (1,)), ((), ())),
        precision=lax.Precision.HIGHEST,
        preferred_element_type=jnp.float32,
    )

    compact = lax.dot_general(
        mine.astype(jnp.bfloat16),
        pick(owner).astype(jnp.bfloat16),
        (((1,), (1,)), ((), ())),
        preferred_element_type=jnp.float32,
    ).astype(jnp.bfloat16)

    @pl.loop(0, early)
    def _(e):
        for slot in range(len(away)):
            early_arrival(slot, e).wait_recv()
            grown[slot, e] = dot(compact, got[slot, e]).astype(jnp.bfloat16)
            grown_copy(slot, e).start()

    for hop in range(1, pairs):
        cross_copy(hop).wait_send()
    for d in others:
        part_copy(d).wait_send()
        sum_copy(d).wait_send()

    @pl.loop(0, early)
    def _(e):
        for slot in range(len(away)):
            early_copy(slot, e).wait_send()
            grown_copy(slot, e).wait()

    @pl.loop(late, units)
    def _(u):
        own_copy(u).wait()
        near_copy(u).wait()

    @pl.loop(0, late)
    def _(u):
        own_copy(u).wait()
        near_copy(u).wait()
        for slot in range(len(away)):
            far_copy(u, slot).wait_send()
            far_arrival(u, slot).wait_recv()


def write(*refs):
    inputs, outputs, held, read_sem, write_sem = refs[:3], refs[3:6], refs[6:9], *refs[9:]
    variables = inputs[0].shape[0]
    parts = [(0, v) for v in range(variables)] + [(1, None), (2, None)]

    def piece(arrays, part):
        ref = arrays[part[0]]
        return ref if part[1] is None else ref.at[part[1]]

    reads = [
        pltpu.make_async_copy(piece(inputs, part), piece(held, part), read_sem.at[i])
        for i, part in enumerate(parts)
    ]
    writes = [
        pltpu.make_async_copy(piece(held, part), piece(outputs, part), write_sem.at[i])
        for i, part in enumerate(parts)
    ]
    for copy in reads:
        copy.start()
    for read, copy in zip(reads, writes):
        read.wait()
        copy.start()
    for copy in writes:
        copy.wait()


def local(snapshots, labels, start, successor):
    count, variables, width = snapshots.shape
    spaces = lax.axis_size("space")
    clusters = lax.axis_size("clus")
    modes = start.shape[1]
    plane = spaces * CORES
    pairs = clusters // CORES
    tall = count // plane
    share = count // clusters
    room = CAP * clusters
    cuts = 3
    units, step = variables * cuts, width // cuts
    away = clusters - CORES
    vmem = pl.BlockSpec(memory_space=pltpu.VMEM)
    hbm = pl.BlockSpec(memory_space=pltpu.HBM)
    dma = pltpu.SemaphoreType.DMA
    results = (
        jax.ShapeDtypeStruct((variables, modes, clusters * width), jnp.bfloat16),
        jax.ShapeDtypeStruct((modes, share), jnp.float32),
        jax.ShapeDtypeStruct((modes, modes), jnp.float32),
    )
    made = pl.pallas_call(
        functools.partial(kernel, (spaces, clusters)),
        out_shape=results,
        in_specs=[hbm] * 4,
        out_specs=(hbm, vmem, vmem),
        scratch_shapes=[
            pltpu.VMEM((variables, count, width), jnp.bfloat16),
            pltpu.VMEM((1, count), jnp.int32),
            pltpu.VMEM((modes, count), jnp.float32),
            pltpu.VMEM((1, clusters), jnp.int32),
            pltpu.VMEM((count, count), jnp.float32),
            pltpu.VMEM((pairs - 1, tall, count), jnp.float32),
            pltpu.VMEM((tall, count), jnp.float32),
            pltpu.VMEM((plane, tall, count), jnp.float32),
            pltpu.VMEM((tall, count), jnp.float32),
            pltpu.VMEM((count, count), jnp.float32),
            pltpu.VMEM((clusters, units, modes, step), jnp.bfloat16),
            pltpu.VMEM((away, EARLY, room, step), jnp.bfloat16),
            pltpu.VMEM((away, EARLY, room, step), jnp.bfloat16),
            pltpu.VMEM((away, EARLY, modes, step), jnp.bfloat16),
            dma((variables,)),
            dma((3,)),
            dma((pairs - 1,)),
            dma((pairs - 1,)),
            dma((plane,)),
            dma((plane,)),
            dma((plane,)),
            dma((plane,)),
            dma((units, clusters)),
            dma((units, clusters)),
            dma((away, EARLY)),
            dma((away, EARLY)),
            dma((units,)),
            dma((away, EARLY)),
        ],
        compiler_params=pltpu.CompilerParams(
            collective_id=0, has_side_effects=True, vmem_limit_bytes=VMEM
        ),
    )(
        jnp.transpose(snapshots, (1, 0, 2)),
        labels.reshape(1, count),
        start.T,
        successor.reshape(1, clusters),
    )
    modes_out, coef, corr = pl.pallas_call(
        write,
        out_shape=results,
        in_specs=[hbm] * 3,
        out_specs=(hbm,) * 3,
        scratch_shapes=[pltpu.VMEM(x.shape, x.dtype) for x in results]
        + [dma((variables + 2,)), dma((variables + 2,))],
        compiler_params=pltpu.CompilerParams(vmem_limit_bytes=VMEM),
    )(*made)
    return jnp.transpose(modes_out, (1, 0, 2))[None], coef.T, corr[None]


def solution(mesh):
    in_specs = (P("groups", None, ("space", "clus")), P("groups"), P("groups", None), P("groups"))
    out_specs = (
        P(("groups", "clus"), None, None, "space"),
        P(("groups", "clus"), None),
        P(("groups", "clus"), None, None),
    )
    return jax.shard_map(local, mesh=mesh, in_specs=in_specs, out_specs=out_specs, check_vma=False)
```

```python
import functools

import jax
import jax.numpy as jnp
from jax import lax
from jax.experimental import pallas as pl
from jax.experimental.pallas import tpu as pltpu
from jax.sharding import PartitionSpec as P

ITERS = 2
CAP = 8
CORES = 2
EARLY = 3
VMEM = 64 * 1024 * 1024
MESH = pl.DeviceIdType.MESH


def split3(x):
    high = x.astype(jnp.bfloat16)
    rest = x - high.astype(jnp.float32)
    middle = rest.astype(jnp.bfloat16)
    low = (rest - middle.astype(jnp.float32)).astype(jnp.bfloat16)
    return high, middle, low


def dot(a, b):
    return jnp.dot(a, b, preferred_element_type=jnp.float32)


def times_gram(rows, pieces, count):
    modes = rows.shape[0]
    parts = dot(jnp.concatenate(split3(rows), axis=0), pieces)
    high = parts[:modes]
    middle = parts[modes : 2 * modes, : 2 * count]
    low = parts[2 * modes :, :count]
    return (
        (high[:, 2 * count :] + middle[:, count:] + low)
        + (high[:, count : 2 * count] + middle[:, :count])
        + high[:, :count]
    )


def orthonormal(rows, same):
    modes, count = rows.shape
    half = modes // 2
    first = [0 if j < half else half for j in range(modes)]
    pairs = jnp.concatenate([rows[j : j + 1] * rows[first[j] :] for j in range(modes)], axis=0)
    total = pairs.shape[0]
    sums = dot(jnp.concatenate(split3(pairs), axis=0), same)
    inner = sums[2 * total :] + sums[total : 2 * total] + sums[:total]
    columns = []
    at = 0
    for j in range(modes):
        height = modes - first[j]
        columns.append(inner[at : at + height])
        at += height
    index = lax.broadcasted_iota(jnp.int32, (modes, count), 0)
    result = jnp.zeros_like(rows)
    rest = rows
    for j in range(modes):
        here = j - first[j]
        scale = lax.rsqrt(columns[j][here : here + 1])
        lower = columns[j] * scale
        solved = rest[j - (modes - rest.shape[0]) :][:1] * scale
        result = jnp.where(index == j, solved, result)
        if j == modes - 1:
            break
        if first[j + 1] != first[j]:
            lower = lower[half:]
            rest = rest[half:]
            shift = half
        else:
            shift = first[j]
        rest = rest - lower * solved
        for n in range(j + 1, modes):
            factor = lower[n - shift : n - shift + 1]
            columns[n] = columns[n] - (lower if first[n] == shift else lower[half:]) * factor
    return result


def kernel(
    sizes,
    snap_hbm,
    labels_hbm,
    start_hbm,
    succ_hbm,
    modes_ref,
    coef_ref,
    corr_ref,
    snap,
    labels_ref,
    start_ref,
    succ_ref,
    partial,
    crossed,
    summed,
    landed,
    chunk,
    gram,
    stage,
    packed,
    got,
    grown,
    load_sem,
    small_sem,
    cross_send,
    cross_recv,
    rs_send,
    rs_recv,
    ag_send,
    ag_recv,
    out_send,
    out_recv,
    early_send,
    early_recv,
    own_sem,
    grown_sem,
):
    spaces, clusters = sizes
    variables, count, width = snap.shape
    modes = start_ref.shape[0]
    devices = spaces * clusters
    plane = spaces * CORES
    tall = count // plane
    units, step = stage.shape[1], stage.shape[3]
    cuts = width // step
    early = packed.shape[1]
    late = units - early
    room = packed.shape[2]
    pairs = clusters // CORES
    owner = lax.axis_index("clus")
    pair, core = owner // CORES, owner % CORES
    space = lax.axis_index("space")
    me = space * CORES + core
    near = pair * CORES + 1 - core
    steps = [(ds, dc) for ds in range(spaces) for dc in range(CORES) if ds + dc]

    def place(d):
        ds, dc = steps[d]
        return lax.rem(space + ds, spaces), 1 - core if dc else core

    def device(d):
        z, c = place(d)
        return {"space": z, "clus": pair * CORES + c}

    def far(hop, c):
        return lax.rem(pair + hop, pairs) * CORES + c

    away = [(hop, c) for hop in range(1, pairs) for c in range(CORES)]

    def load(v):
        return pltpu.make_async_copy(snap_hbm.at[v], snap.at[v], load_sem.at[v])

    small = [
        pltpu.make_async_copy(source, target, small_sem.at[i])
        for i, (source, target) in enumerate(
            ((labels_hbm, labels_ref), (start_hbm, start_ref), (succ_hbm, succ_ref))
        )
    ]
    for copy in small:
        copy.start()
    for v in (variables - 1, *range(variables - 1)):
        load(v).start()
    barrier = pltpu.get_barrier_semaphore()

    for hop, c in away:
        pl.semaphore_signal(barrier, inc=1, device_id={"clus": far(hop, c)}, device_id_type=MESH)

    for d in range(len(steps)):
        pl.semaphore_signal(barrier, inc=1, device_id=device(d), device_id_type=MESH)

    for copy in small:
        copy.wait()
    label_row = labels_ref[...]
    wide = jnp.broadcast_to(label_row.astype(jnp.float32), (count, count))
    same = (wide == wide.T).astype(jnp.bfloat16)
    before = lax.broadcasted_iota(jnp.int32, (count, count), 0) < lax.broadcasted_iota(
        jnp.int32, (count, count), 1
    )
    rank = dot(
        jnp.ones((16, count), jnp.bfloat16),
        jnp.where(before, same.astype(jnp.float32), 0.0).astype(jnp.bfloat16),
    )[:1].astype(jnp.int32)
    slots = lax.broadcasted_iota(jnp.int32, (room, count), 0)

    def pick(cluster):
        return jnp.where((slots == rank) & (label_row == cluster), 1.0, 0.0)

    def early_copy(slot, e):
        hop, c = away[slot]
        return pltpu.make_async_remote_copy(
            src_ref=packed.at[slot, e],
            dst_ref=got.at[(hop - 1) * CORES + core, e],
            send_sem=early_send.at[slot, e],
            recv_sem=early_recv.at[(hop - 1) * CORES + core, e],
            device_id={"clus": far(hop, c)},
            device_id_type=MESH,
        )

    def early_arrival(slot, e):
        return pltpu.make_async_remote_copy(
            src_ref=packed.at[slot, e],
            dst_ref=got.at[slot, e],
            send_sem=early_send.at[slot, e],
            recv_sem=early_recv.at[slot, e],
            device_id={"clus": far(*away[slot])},
            device_id_type=MESH,
        )

    def cells_of(u):
        return u // cuts, pl.ds(pl.multiple_of((u % cuts) * step, step), step)

    def spot(u, source):
        start = pl.multiple_of(source * width + (u % cuts) * step, step)
        return modes_ref.at[u // cuts, :, pl.ds(start, step)]

    picks = jnp.concatenate([pick(far(hop, c)) for hop, c in away], axis=0).astype(jnp.bfloat16)

    def send_early(low, high):
        @pl.loop(low, high)
        def _(e):
            v, cells = cells_of(late + e)
            made = dot(picks, snap[v, :, cells]).astype(jnp.bfloat16)
            for slot in range(len(away)):
                packed[slot, e] = made[slot * room : (slot + 1) * room]
            for slot in range(len(away)):
                early_copy(slot, e).start()

    partial[...] = jnp.zeros_like(partial)

    def add_gram(low, high):
        @pl.loop(low, high)
        def _(turn):
            v = lax.rem(turn + variables - 1, variables)
            load(v).wait()
            block = snap[v]
            partial[...] += lax.dot_general(
                block, block, (((1,), (1,)), ((), ())), preferred_element_type=jnp.float32
            )

    def part_copy(d):
        z, c = place(d)
        rows = pl.ds(pl.multiple_of((z * CORES + c) * tall, tall), tall)
        return pltpu.make_async_remote_copy(
            src_ref=partial.at[rows],
            dst_ref=landed.at[d],
            send_sem=rs_send.at[d],
            recv_sem=rs_recv.at[d],
            device_id=device(d),
            device_id_type=MESH,
        )

    def cross_copy(hop):
        return pltpu.make_async_remote_copy(
            src_ref=chunk,
            dst_ref=crossed.at[hop - 1],
            send_sem=cross_send.at[hop - 1],
            recv_sem=cross_recv.at[hop - 1],
            device_id={"clus": far(hop, core)},
            device_id_type=MESH,
        )

    own = pl.ds(pl.multiple_of(me * tall, tall), tall)

    def sum_copy(d):
        return pltpu.make_async_remote_copy(
            src_ref=summed,
            dst_ref=gram.at[own],
            send_sem=ag_send.at[d],
            recv_sem=ag_recv.at[d],
            device_id=device(d),
            device_id_type=MESH,
        )

    others = range(len(steps))
    first = variables - 2
    add_gram(0, first)
    pl.semaphore_wait(barrier, len(steps) + len(away))
    send_early(early - 1, early)
    add_gram(first, variables)
    for d in others:
        part_copy(d).start()
    send_early(0, 1)

    total = partial[own]
    for d in others:
        part_copy(d).wait_recv()
        total = total + landed[d]
    chunk[...] = total
    for hop in range(1, pairs):
        cross_copy(hop).start()
    send_early(1, early - 1)
    for hop in range(1, pairs):
        cross_copy(hop).wait_recv()
        total = total + crossed[hop - 1]
    total = total * (1.0 / (variables * width * devices))
    summed[...] = total
    gram[own] = total
    for d in others:
        sum_copy(d).start()
    for d in others:
        sum_copy(d).wait_recv()

    pieces = split3(gram[...])
    masked = jnp.concatenate([same * piece for piece in pieces], axis=1)
    basis = start_ref[...]
    for _ in range(ITERS):
        image = times_gram(basis, masked, count) + basis
        basis = orthonormal(image, same)

    keep = basis.astype(jnp.bfloat16).astype(jnp.float32)
    left = jnp.concatenate(
        [jnp.where(label_row == k, keep, 0.0) for k in range(clusters)], axis=0
    ).astype(jnp.bfloat16)

    def mode_copy(u, target, slot_out, slot_in):
        return pltpu.make_async_remote_copy(
            src_ref=stage.at[target, u],
            dst_ref=spot(u, owner),
            send_sem=out_send.at[u, slot_out],
            recv_sem=out_recv.at[u, slot_in],
            device_id={"clus": target},
            device_id_type=MESH,
        )

    def near_copy(u):
        return mode_copy(u, near, 0, 0)

    def far_copy(u, slot):
        hop, c = away[slot]
        return mode_copy(u, far(hop, c), 1 + slot, 1 + (hop - 1) * CORES + core)

    def far_arrival(u, slot):
        return mode_copy(u, far(*away[slot]), 1 + slot, 1 + slot)

    def own_copy(u):
        return pltpu.make_async_copy(stage.at[owner, u], spot(u, owner), own_sem.at[u])

    def grown_copy(slot, e):
        source = lax.rem(pair + pairs - away[slot][0], pairs) * CORES + away[slot][1]
        return pltpu.make_async_copy(
            grown.at[slot, e], spot(late + e, source), grown_sem.at[slot, e]
        )

    def make(u):
        v, cells = cells_of(u)
        made = dot(left, snap[v, :, cells]).astype(jnp.bfloat16)
        for k in range(clusters):
            stage[k, u] = made[k * modes : (k + 1) * modes]

    @pl.loop(0, late)
    def _(u):
        make(u)
        for slot in range(len(away)):
            far_copy(u, slot).start()
        near_copy(u).start()
        own_copy(u).start()

    @pl.loop(late, units)
    def _(u):
        make(u)
        near_copy(u).start()
        own_copy(u).start()

    share = coef_ref.shape[1]
    picked = jnp.zeros((modes, share), jnp.float32)
    for k in range(clusters):
        picked = jnp.where(owner == k, basis[:, k * share : (k + 1) * share], picked)
    coef_ref[...] = picked
    is_own = lax.broadcasted_iota(jnp.int32, (1, clusters), 1) == owner
    follower = jnp.sum(jnp.where(is_own, succ_ref[...], 0), axis=1, keepdims=True)
    mine = jnp.where(label_row == owner, keep, 0.0)
    other = jnp.where(label_row == follower, keep, 0.0).astype(jnp.bfloat16)
    parts = dot(other, jnp.concatenate(pieces, axis=1))
    image = parts[:, 2 * count :] + parts[:, count : 2 * count] + parts[:, :count]
    corr_ref[...] = lax.dot_general(
        mine,
        image,
        (((1,), (1,)), ((), ())),
        precision=lax.Precision.HIGHEST,
        preferred_element_type=jnp.float32,
    )

    compact = lax.dot_general(
        mine.astype(jnp.bfloat16),
        pick(owner).astype(jnp.bfloat16),
        (((1,), (1,)), ((), ())),
        preferred_element_type=jnp.float32,
    ).astype(jnp.bfloat16)

    @pl.loop(0, early)
    def _(e):
        for slot in range(len(away)):
            early_arrival(slot, e).wait_recv()
            grown[slot, e] = dot(compact, got[slot, e]).astype(jnp.bfloat16)
            grown_copy(slot, e).start()

    for hop in range(1, pairs):
        cross_copy(hop).wait_send()
    for d in others:
        part_copy(d).wait_send()
        sum_copy(d).wait_send()

    @pl.loop(0, early)
    def _(e):
        for slot in range(len(away)):
            early_copy(slot, e).wait_send()
            grown_copy(slot, e).wait()

    @pl.loop(late, units)
    def _(u):
        own_copy(u).wait()
        near_copy(u).wait()

    @pl.loop(0, late)
    def _(u):
        own_copy(u).wait()
        near_copy(u).wait()
        for slot in range(len(away)):
            far_copy(u, slot).wait_send()
            far_arrival(u, slot).wait_recv()


def write(*refs):
    inputs, outputs, held, read_sem, write_sem = refs[:3], refs[3:6], refs[6:9], *refs[9:]
    variables = inputs[0].shape[0]
    parts = [(0, v) for v in range(variables)] + [(1, None), (2, None)]

    def piece(arrays, part):
        ref = arrays[part[0]]
        return ref if part[1] is None else ref.at[part[1]]

    reads = [
        pltpu.make_async_copy(piece(inputs, part), piece(held, part), read_sem.at[i])
        for i, part in enumerate(parts)
    ]
    writes = [
        pltpu.make_async_copy(piece(held, part), piece(outputs, part), write_sem.at[i])
        for i, part in enumerate(parts)
    ]
    for copy in reads:
        copy.start()
    for read, copy in zip(reads, writes):
        read.wait()
        copy.start()
    for copy in writes:
        copy.wait()


def local(snapshots, labels, start, successor):
    count, variables, width = snapshots.shape
    spaces = lax.axis_size("space")
    clusters = lax.axis_size("clus")
    modes = start.shape[1]
    plane = spaces * CORES
    pairs = clusters // CORES
    tall = count // plane
    share = count // clusters
    room = CAP * clusters
    cuts = 3
    units, step = variables * cuts, width // cuts
    away = clusters - CORES
    vmem = pl.BlockSpec(memory_space=pltpu.VMEM)
    hbm = pl.BlockSpec(memory_space=pltpu.HBM)
    dma = pltpu.SemaphoreType.DMA
    results = (
        jax.ShapeDtypeStruct((variables, modes, clusters * width), jnp.bfloat16),
        jax.ShapeDtypeStruct((modes, share), jnp.float32),
        jax.ShapeDtypeStruct((modes, modes), jnp.float32),
    )
    made = pl.pallas_call(
        functools.partial(kernel, (spaces, clusters)),
        out_shape=results,
        in_specs=[hbm] * 4,
        out_specs=(hbm, vmem, vmem),
        scratch_shapes=[
            pltpu.VMEM((variables, count, width), jnp.bfloat16),
            pltpu.VMEM((1, count), jnp.int32),
            pltpu.VMEM((modes, count), jnp.float32),
            pltpu.VMEM((1, clusters), jnp.int32),
            pltpu.VMEM((count, count), jnp.float32),
            pltpu.VMEM((pairs - 1, tall, count), jnp.float32),
            pltpu.VMEM((tall, count), jnp.float32),
            pltpu.VMEM((plane, tall, count), jnp.float32),
            pltpu.VMEM((tall, count), jnp.float32),
            pltpu.VMEM((count, count), jnp.float32),
            pltpu.VMEM((clusters, units, modes, step), jnp.bfloat16),
            pltpu.VMEM((away, EARLY, room, step), jnp.bfloat16),
            pltpu.VMEM((away, EARLY, room, step), jnp.bfloat16),
            pltpu.VMEM((away, EARLY, modes, step), jnp.bfloat16),
            dma((variables,)),
            dma((3,)),
            dma((pairs - 1,)),
            dma((pairs - 1,)),
            dma((plane,)),
            dma((plane,)),
            dma((plane,)),
            dma((plane,)),
            dma((units, clusters)),
            dma((units, clusters)),
            dma((away, EARLY)),
            dma((away, EARLY)),
            dma((units,)),
            dma((away, EARLY)),
        ],
        compiler_params=pltpu.CompilerParams(
            collective_id=0, has_side_effects=True, vmem_limit_bytes=VMEM
        ),
    )(
        jnp.transpose(snapshots, (1, 0, 2)),
        labels.reshape(1, count),
        start.T,
        successor.reshape(1, clusters),
    )
    modes_out, coef, corr = pl.pallas_call(
        write,
        out_shape=results,
        in_specs=[hbm] * 3,
        out_specs=(hbm,) * 3,
        scratch_shapes=[pltpu.VMEM(x.shape, x.dtype) for x in results]
        + [dma((variables + 2,)), dma((variables + 2,))],
        compiler_params=pltpu.CompilerParams(vmem_limit_bytes=VMEM),
    )(*made)
    return jnp.transpose(modes_out, (1, 0, 2))[None], coef.T, corr[None]


def solution(mesh):
    in_specs = (P("groups", None, ("space", "clus")), P("groups"), P("groups", None), P("groups"))
    out_specs = (
        P(("groups", "clus"), None, None, "space"),
        P(("groups", "clus"), None),
        P(("groups", "clus"), None, None),
    )
    return jax.shard_map(local, mesh=mesh, in_specs=in_specs, out_specs=out_specs, check_vma=False)
```

```python
import functools

import jax
import jax.numpy as jnp
from jax import lax
from jax.experimental import pallas as pl
from jax.experimental.pallas import tpu as pltpu
from jax.sharding import PartitionSpec as P

ITERS = 2
CAP = 8
CORES = 2
EARLY = 4
VMEM = 64 * 1024 * 1024
MESH = pl.DeviceIdType.MESH


def split3(x):
    high = x.astype(jnp.bfloat16)
    rest = x - high.astype(jnp.float32)
    middle = rest.astype(jnp.bfloat16)
    low = (rest - middle.astype(jnp.float32)).astype(jnp.bfloat16)
    return high, middle, low


def dot(a, b):
    return jnp.dot(a, b, preferred_element_type=jnp.float32)


def times_gram(rows, pieces, count):
    modes = rows.shape[0]
    parts = dot(jnp.concatenate(split3(rows), axis=0), pieces)
    high = parts[:modes]
    middle = parts[modes : 2 * modes, : 2 * count]
    low = parts[2 * modes :, :count]
    return (
        (high[:, 2 * count :] + middle[:, count:] + low)
        + (high[:, count : 2 * count] + middle[:, :count])
        + high[:, :count]
    )


def orthonormal(rows, same):
    modes, count = rows.shape
    half = modes // 2
    first = [0 if j < half else half for j in range(modes)]
    pairs = jnp.concatenate([rows[j : j + 1] * rows[first[j] :] for j in range(modes)], axis=0)
    total = pairs.shape[0]
    sums = dot(jnp.concatenate(split3(pairs), axis=0), same)
    inner = sums[2 * total :] + sums[total : 2 * total] + sums[:total]
    columns = []
    at = 0
    for j in range(modes):
        height = modes - first[j]
        columns.append(inner[at : at + height])
        at += height
    index = lax.broadcasted_iota(jnp.int32, (modes, count), 0)
    result = jnp.zeros_like(rows)
    rest = rows
    for j in range(modes):
        here = j - first[j]
        scale = lax.rsqrt(columns[j][here : here + 1])
        lower = columns[j] * scale
        solved = rest[j - (modes - rest.shape[0]) :][:1] * scale
        result = jnp.where(index == j, solved, result)
        if j == modes - 1:
            break
        if first[j + 1] != first[j]:
            lower = lower[half:]
            rest = rest[half:]
            shift = half
        else:
            shift = first[j]
        rest = rest - lower * solved
        for n in range(j + 1, modes):
            factor = lower[n - shift : n - shift + 1]
            columns[n] = columns[n] - (lower if first[n] == shift else lower[half:]) * factor
    return result


def kernel(
    sizes,
    snap_hbm,
    labels_hbm,
    start_hbm,
    succ_hbm,
    modes_ref,
    coef_ref,
    corr_ref,
    snap,
    labels_ref,
    start_ref,
    succ_ref,
    partial,
    crossed,
    summed,
    landed,
    chunk,
    gram,
    stage,
    packed,
    got,
    grown,
    load_sem,
    small_sem,
    cross_send,
    cross_recv,
    rs_send,
    rs_recv,
    ag_send,
    ag_recv,
    out_send,
    out_recv,
    early_send,
    early_recv,
    own_sem,
    grown_sem,
):
    spaces, clusters = sizes
    variables, count, width = snap.shape
    modes = start_ref.shape[0]
    devices = spaces * clusters
    plane = spaces * CORES
    tall = count // plane
    units, step = stage.shape[1], stage.shape[3]
    cuts = width // step
    early = packed.shape[1]
    late = units - early
    room = packed.shape[2]
    pairs = clusters // CORES
    owner = lax.axis_index("clus")
    pair, core = owner // CORES, owner % CORES
    me = lax.axis_index("space") * CORES + core

    def place(index):
        return {"space": index // CORES, "clus": pair * CORES + index % CORES}

    def far(hop, c):
        return lax.rem(pair + hop, pairs) * CORES + c

    away = [(hop, c) for hop in range(1, pairs) for c in range(CORES)]

    def load(v):
        return pltpu.make_async_copy(snap_hbm.at[v], snap.at[v], load_sem.at[v])

    small = [
        pltpu.make_async_copy(source, target, small_sem.at[i])
        for i, (source, target) in enumerate(
            ((labels_hbm, labels_ref), (start_hbm, start_ref), (succ_hbm, succ_ref))
        )
    ]
    for v in range(variables):
        load(v).start()
    for copy in small:
        copy.start()
    barrier = pltpu.get_barrier_semaphore()

    for hop, c in away:
        pl.semaphore_signal(barrier, inc=1, device_id={"clus": far(hop, c)}, device_id_type=MESH)

    @pl.loop(1, plane)
    def _(d):
        target = lax.rem(me + d, plane)
        pl.semaphore_signal(barrier, inc=1, device_id=place(target), device_id_type=MESH)

    partial[...] = jnp.zeros_like(partial)

    @pl.loop(0, variables)
    def _(v):
        load(v).wait()
        part = width // 2
        halves = []
        for h in range(2):
            block = snap[v, :, h * part : (h + 1) * part]
            halves.append(
                lax.dot_general(
                    block, block, (((1,), (1,)), ((), ())), preferred_element_type=jnp.float32
                )
            )
        partial[...] += halves[0] + halves[1]

    pl.semaphore_wait(barrier, plane - 1 + len(away))

    def cross_copy(hop):
        return pltpu.make_async_remote_copy(
            src_ref=partial,
            dst_ref=crossed.at[hop - 1],
            send_sem=cross_send.at[hop - 1],
            recv_sem=cross_recv.at[hop - 1],
            device_id={"clus": far(hop, core)},
            device_id_type=MESH,
        )

    for hop in range(1, pairs):
        cross_copy(hop).start()

    def part_copy(d):
        target = lax.rem(me + d, plane)
        rows = pl.ds(pl.multiple_of(target * tall, tall), tall)
        return pltpu.make_async_remote_copy(
            src_ref=summed.at[rows],
            dst_ref=landed.at[d],
            send_sem=rs_send.at[d],
            recv_sem=rs_recv.at[d],
            device_id=place(target),
            device_id_type=MESH,
        )

    def sum_copy(d):
        target = lax.rem(me + d, plane)
        rows = pl.ds(pl.multiple_of(me * tall, tall), tall)
        return pltpu.make_async_remote_copy(
            src_ref=chunk,
            dst_ref=gram.at[rows],
            send_sem=ag_send.at[d],
            recv_sem=ag_recv.at[d],
            device_id=place(target),
            device_id_type=MESH,
        )

    for copy in small:
        copy.wait()
    label_row = labels_ref[...]
    wide = jnp.broadcast_to(label_row.astype(jnp.float32), (count, count))
    same = (wide == wide.T).astype(jnp.bfloat16)
    before = lax.broadcasted_iota(jnp.int32, (count, count), 0) < lax.broadcasted_iota(
        jnp.int32, (count, count), 1
    )
    rank = dot(
        jnp.ones((16, count), jnp.bfloat16),
        jnp.where(before, same.astype(jnp.float32), 0.0).astype(jnp.bfloat16),
    )[:1].astype(jnp.int32)
    slots = lax.broadcasted_iota(jnp.int32, (room, count), 0)

    def pick(cluster):
        return jnp.where((slots == rank) & (label_row == cluster), 1.0, 0.0)

    def early_copy(slot, e):
        hop, c = away[slot]
        return pltpu.make_async_remote_copy(
            src_ref=packed.at[slot, e],
            dst_ref=got.at[(hop - 1) * CORES + core, e],
            send_sem=early_send.at[slot, e],
            recv_sem=early_recv.at[(hop - 1) * CORES + core, e],
            device_id={"clus": far(hop, c)},
            device_id_type=MESH,
        )

    def early_arrival(slot, e):
        return pltpu.make_async_remote_copy(
            src_ref=packed.at[slot, e],
            dst_ref=got.at[slot, e],
            send_sem=early_send.at[slot, e],
            recv_sem=early_recv.at[slot, e],
            device_id={"clus": far(*away[slot])},
            device_id_type=MESH,
        )

    def cells_of(u):
        return u // cuts, pl.ds(pl.multiple_of((u % cuts) * step, step), step)

    def spot(u, source):
        start = pl.multiple_of(source * width + (u % cuts) * step, step)
        return modes_ref.at[u // cuts, :, pl.ds(start, step)]

    picks = jnp.concatenate([pick(far(hop, c)) for hop, c in away], axis=0).astype(jnp.bfloat16)

    def send_early(low, high):
        @pl.loop(low, high)
        def _(e):
            v, cells = cells_of(late + e)
            made = dot(picks, snap[v, :, cells]).astype(jnp.bfloat16)
            for slot in range(len(away)):
                packed[slot, e] = made[slot * room : (slot + 1) * room]
            for slot in range(len(away)):
                early_copy(slot, e).start()

    ahead = (early + 1) // 2
    send_early(0, ahead)

    for hop in range(1, pairs):
        cross_copy(hop).wait_recv()
    total = partial[...]
    for hop in range(1, pairs):
        total = total + crossed[hop - 1]
    summed[...] = total

    @pl.loop(1, plane)
    def _(d):
        part_copy(d).start()

    send_early(ahead, early)

    own = pl.ds(pl.multiple_of(me * tall, tall), tall)

    def add(d, total):
        part_copy(d).wait_recv()
        return total + landed[d]

    total = lax.fori_loop(1, plane, add, summed[own])
    total = total * (1.0 / (variables * width * devices))
    chunk[...] = total
    gram[own] = total

    @pl.loop(1, plane)
    def _(d):
        sum_copy(d).start()

    @pl.loop(1, plane)
    def _(d):
        sum_copy(d).wait_recv()

    pieces = split3(gram[...])
    masked = jnp.concatenate([same * piece for piece in pieces], axis=1)
    basis = start_ref[...]
    for _ in range(ITERS):
        image = times_gram(basis, masked, count) + basis
        basis = orthonormal(image, same)

    keep = basis.astype(jnp.bfloat16).astype(jnp.float32)
    left = jnp.concatenate(
        [jnp.where(label_row == k, keep, 0.0) for k in range(clusters)], axis=0
    ).astype(jnp.bfloat16)

    def mode_copy(u, d):
        target = lax.rem(owner + d, clusters)
        return pltpu.make_async_remote_copy(
            src_ref=stage.at[target, u],
            dst_ref=spot(u, owner),
            send_sem=out_send.at[u, d],
            recv_sem=out_recv.at[u, d],
            device_id={"clus": target},
            device_id_type=MESH,
        )

    def own_copy(u):
        return pltpu.make_async_copy(stage.at[owner, u], spot(u, owner), own_sem.at[u])

    def grown_copy(slot, e):
        source = lax.rem(pair + pairs - away[slot][0], pairs) * CORES + away[slot][1]
        return pltpu.make_async_copy(
            grown.at[slot, e], spot(late + e, source), grown_sem.at[slot, e]
        )

    def make(u):
        v, cells = cells_of(u)
        made = dot(left, snap[v, :, cells]).astype(jnp.bfloat16)
        for k in range(clusters):
            stage[k, u] = made[k * modes : (k + 1) * modes]

    def is_near(d):
        return (owner + d) % clusters // CORES == pair

    @pl.loop(0, late)
    def _(u):
        make(u)
        for d in range(1, clusters):
            mode_copy(u, d).start()
        own_copy(u).start()

    @pl.loop(late, units)
    def _(u):
        make(u)
        for d in range(1, clusters):
            pl.when(is_near(d))(lambda d=d: mode_copy(u, d).start())
        own_copy(u).start()

    share = coef_ref.shape[1]
    picked = jnp.zeros((modes, share), jnp.float32)
    for k in range(clusters):
        picked = jnp.where(owner == k, basis[:, k * share : (k + 1) * share], picked)
    coef_ref[...] = picked
    is_own = lax.broadcasted_iota(jnp.int32, (1, clusters), 1) == owner
    follower = jnp.sum(jnp.where(is_own, succ_ref[...], 0), axis=1, keepdims=True)
    mine = jnp.where(label_row == owner, keep, 0.0)
    other = jnp.where(label_row == follower, keep, 0.0).astype(jnp.bfloat16)
    parts = dot(other, jnp.concatenate(pieces, axis=1))
    image = parts[:, 2 * count :] + parts[:, count : 2 * count] + parts[:, :count]
    corr_ref[...] = lax.dot_general(
        mine,
        image,
        (((1,), (1,)), ((), ())),
        precision=lax.Precision.HIGHEST,
        preferred_element_type=jnp.float32,
    )

    compact = lax.dot_general(
        mine.astype(jnp.bfloat16),
        pick(owner).astype(jnp.bfloat16),
        (((1,), (1,)), ((), ())),
        preferred_element_type=jnp.float32,
    ).astype(jnp.bfloat16)

    @pl.loop(0, early)
    def _(e):
        for slot in range(len(away)):
            early_arrival(slot, e).wait_recv()
            grown[slot, e] = dot(compact, got[slot, e]).astype(jnp.bfloat16)
            grown_copy(slot, e).start()

    for hop in range(1, pairs):
        cross_copy(hop).wait_send()

    @pl.loop(1, plane)
    def _(d):
        part_copy(d).wait_send()
        sum_copy(d).wait_send()

    @pl.loop(0, early)
    def _(e):
        for slot in range(len(away)):
            early_copy(slot, e).wait_send()
            grown_copy(slot, e).wait()

    @pl.loop(late, units)
    def _(u):
        own_copy(u).wait()
        for d in range(1, clusters):
            pl.when(is_near(d))(lambda d=d: mode_copy(u, d).wait_send())
            pl.when((owner + clusters - d) % clusters // CORES == pair)(
                lambda d=d: mode_copy(u, d).wait_recv()
            )

    @pl.loop(0, late)
    def _(u):
        own_copy(u).wait()
        for d in range(1, clusters):
            mode_copy(u, d).wait()


def write(*refs):
    inputs, outputs, held, read_sem, write_sem = refs[:3], refs[3:6], refs[6:9], *refs[9:]
    variables = inputs[0].shape[0]
    parts = [(0, v) for v in range(variables)] + [(1, None), (2, None)]

    def piece(arrays, part):
        ref = arrays[part[0]]
        return ref if part[1] is None else ref.at[part[1]]

    reads = [
        pltpu.make_async_copy(piece(inputs, part), piece(held, part), read_sem.at[i])
        for i, part in enumerate(parts)
    ]
    writes = [
        pltpu.make_async_copy(piece(held, part), piece(outputs, part), write_sem.at[i])
        for i, part in enumerate(parts)
    ]
    for copy in reads:
        copy.start()
    for read, copy in zip(reads, writes):
        read.wait()
        copy.start()
    for copy in writes:
        copy.wait()


def local(snapshots, labels, start, successor):
    count, variables, width = snapshots.shape
    spaces = lax.axis_size("space")
    clusters = lax.axis_size("clus")
    modes = start.shape[1]
    plane = spaces * CORES
    pairs = clusters // CORES
    tall = count // plane
    share = count // clusters
    room = CAP * clusters
    cuts = 3
    units, step = variables * cuts, width // cuts
    away = clusters - CORES
    vmem = pl.BlockSpec(memory_space=pltpu.VMEM)
    hbm = pl.BlockSpec(memory_space=pltpu.HBM)
    dma = pltpu.SemaphoreType.DMA
    results = (
        jax.ShapeDtypeStruct((variables, modes, clusters * width), jnp.bfloat16),
        jax.ShapeDtypeStruct((modes, share), jnp.float32),
        jax.ShapeDtypeStruct((modes, modes), jnp.float32),
    )
    made = pl.pallas_call(
        functools.partial(kernel, (spaces, clusters)),
        out_shape=results,
        in_specs=[hbm] * 4,
        out_specs=(hbm, vmem, vmem),
        scratch_shapes=[
            pltpu.VMEM((variables, count, width), jnp.bfloat16),
            pltpu.VMEM((1, count), jnp.int32),
            pltpu.VMEM((modes, count), jnp.float32),
            pltpu.VMEM((1, clusters), jnp.int32),
            pltpu.VMEM((count, count), jnp.float32),
            pltpu.VMEM((pairs - 1, count, count), jnp.float32),
            pltpu.VMEM((count, count), jnp.float32),
            pltpu.VMEM((plane, tall, count), jnp.float32),
            pltpu.VMEM((tall, count), jnp.float32),
            pltpu.VMEM((count, count), jnp.float32),
            pltpu.VMEM((clusters, units, modes, step), jnp.bfloat16),
            pltpu.VMEM((away, EARLY, room, step), jnp.bfloat16),
            pltpu.VMEM((away, EARLY, room, step), jnp.bfloat16),
            pltpu.VMEM((away, EARLY, modes, step), jnp.bfloat16),
            dma((variables,)),
            dma((3,)),
            dma((pairs - 1,)),
            dma((pairs - 1,)),
            dma((plane,)),
            dma((plane,)),
            dma((plane,)),
            dma((plane,)),
            dma((units, clusters)),
            dma((units, clusters)),
            dma((away, EARLY)),
            dma((away, EARLY)),
            dma((units,)),
            dma((away, EARLY)),
        ],
        compiler_params=pltpu.CompilerParams(
            collective_id=0, has_side_effects=True, vmem_limit_bytes=VMEM
        ),
    )(
        jnp.transpose(snapshots, (1, 0, 2)),
        labels.reshape(1, count),
        start.T,
        successor.reshape(1, clusters),
    )
    modes_out, coef, corr = pl.pallas_call(
        write,
        out_shape=results,
        in_specs=[hbm] * 3,
        out_specs=(hbm,) * 3,
        scratch_shapes=[pltpu.VMEM(x.shape, x.dtype) for x in results]
        + [dma((variables + 2,)), dma((variables + 2,))],
        compiler_params=pltpu.CompilerParams(vmem_limit_bytes=VMEM),
    )(*made)
    return jnp.transpose(modes_out, (1, 0, 2))[None], coef.T, corr[None]


def solution(mesh):
    in_specs = (P("groups", None, ("space", "clus")), P("groups"), P("groups", None), P("groups"))
    out_specs = (
        P(("groups", "clus"), None, None, "space"),
        P(("groups", "clus"), None),
        P(("groups", "clus"), None, None),
    )
    return jax.shard_map(local, mesh=mesh, in_specs=in_specs, out_specs=out_specs, check_vma=False)
```

```python
import functools

import jax
import jax.numpy as jnp
from jax import lax
from jax.experimental import pallas as pl
from jax.experimental.pallas import tpu as pltpu
from jax.sharding import PartitionSpec as P

ITERS = 2
CAP = 8
CORES = 2
EARLY = 4
VMEM = 64 * 1024 * 1024
MESH = pl.DeviceIdType.MESH


def split3(x):
    high = x.astype(jnp.bfloat16)
    rest = x - high.astype(jnp.float32)
    middle = rest.astype(jnp.bfloat16)
    low = (rest - middle.astype(jnp.float32)).astype(jnp.bfloat16)
    return high, middle, low


def dot(a, b):
    return jnp.dot(a, b, preferred_element_type=jnp.float32)


def times_gram(rows, pieces, count):
    modes = rows.shape[0]
    parts = dot(jnp.concatenate(split3(rows), axis=0), pieces)
    high = parts[:modes]
    middle = parts[modes : 2 * modes, : 2 * count]
    low = parts[2 * modes :, :count]
    return (
        (high[:, 2 * count :] + middle[:, count:] + low)
        + (high[:, count : 2 * count] + middle[:, :count])
        + high[:, :count]
    )


def orthonormal(rows, same):
    modes, count = rows.shape
    half = modes // 2
    first = [0 if j < half else half for j in range(modes)]
    pairs = jnp.concatenate([rows[j : j + 1] * rows[first[j] :] for j in range(modes)], axis=0)
    total = pairs.shape[0]
    sums = dot(jnp.concatenate(split3(pairs), axis=0), same)
    inner = sums[2 * total :] + sums[total : 2 * total] + sums[:total]
    columns = []
    at = 0
    for j in range(modes):
        height = modes - first[j]
        columns.append(inner[at : at + height])
        at += height
    index = lax.broadcasted_iota(jnp.int32, (modes, count), 0)
    result = jnp.zeros_like(rows)
    rest = rows
    for j in range(modes):
        here = j - first[j]
        scale = lax.rsqrt(columns[j][here : here + 1])
        lower = columns[j] * scale
        solved = rest[j - (modes - rest.shape[0]) :][:1] * scale
        result = jnp.where(index == j, solved, result)
        if j == modes - 1:
            break
        if first[j + 1] != first[j]:
            lower = lower[half:]
            rest = rest[half:]
            shift = half
        else:
            shift = first[j]
        rest = rest - lower * solved
        for n in range(j + 1, modes):
            factor = lower[n - shift : n - shift + 1]
            columns[n] = columns[n] - (lower if first[n] == shift else lower[half:]) * factor
    return result


def kernel(
    sizes,
    snap_hbm,
    labels_hbm,
    start_hbm,
    succ_hbm,
    modes_ref,
    coef_ref,
    corr_ref,
    snap,
    labels_ref,
    start_ref,
    succ_ref,
    partial,
    crossed,
    summed,
    landed,
    chunk,
    gram,
    stage,
    packed,
    got,
    grown,
    load_sem,
    small_sem,
    cross_send,
    cross_recv,
    rs_send,
    rs_recv,
    ag_send,
    ag_recv,
    out_send,
    out_recv,
    early_send,
    early_recv,
    own_sem,
    grown_sem,
):
    spaces, clusters = sizes
    variables, count, width = snap.shape
    modes = start_ref.shape[0]
    devices = spaces * clusters
    plane = spaces * CORES
    tall = count // plane
    units, step = stage.shape[1], stage.shape[3]
    cuts = width // step
    early = packed.shape[1]
    late = units - early
    room = packed.shape[2]
    pairs = clusters // CORES
    owner = lax.axis_index("clus")
    pair, core = owner // CORES, owner % CORES
    space = lax.axis_index("space")
    me = space * CORES + core
    near = pair * CORES + 1 - core
    steps = [(ds, dc) for ds in range(spaces) for dc in range(CORES) if ds + dc]

    def place(d):
        ds, dc = steps[d]
        return lax.rem(space + ds, spaces), 1 - core if dc else core

    def device(d):
        z, c = place(d)
        return {"space": z, "clus": pair * CORES + c}

    def far(hop, c):
        return lax.rem(pair + hop, pairs) * CORES + c

    away = [(hop, c) for hop in range(1, pairs) for c in range(CORES)]

    def load(v):
        return pltpu.make_async_copy(snap_hbm.at[v], snap.at[v], load_sem.at[v])

    small = [
        pltpu.make_async_copy(source, target, small_sem.at[i])
        for i, (source, target) in enumerate(
            ((labels_hbm, labels_ref), (start_hbm, start_ref), (succ_hbm, succ_ref))
        )
    ]
    for copy in small:
        copy.start()
    for v in (variables - 1, *range(variables - 1)):
        load(v).start()
    barrier = pltpu.get_barrier_semaphore()

    for hop, c in away:
        pl.semaphore_signal(barrier, inc=1, device_id={"clus": far(hop, c)}, device_id_type=MESH)

    for d in range(len(steps)):
        pl.semaphore_signal(barrier, inc=1, device_id=device(d), device_id_type=MESH)

    partial[...] = jnp.zeros_like(partial)

    def add_gram(low, high):
        @pl.loop(low, high)
        def _(turn):
            v = lax.rem(turn + variables - 1, variables)
            load(v).wait()
            block = snap[v]
            partial[...] += lax.dot_general(
                block, block, (((1,), (1,)), ((), ())), preferred_element_type=jnp.float32
            )

    def part_copy(d):
        z, c = place(d)
        rows = pl.ds(pl.multiple_of((z * CORES + c) * tall, tall), tall)
        return pltpu.make_async_remote_copy(
            src_ref=partial.at[rows],
            dst_ref=landed.at[d],
            send_sem=rs_send.at[d],
            recv_sem=rs_recv.at[d],
            device_id=device(d),
            device_id_type=MESH,
        )

    def cross_copy(hop):
        return pltpu.make_async_remote_copy(
            src_ref=chunk,
            dst_ref=crossed.at[hop - 1],
            send_sem=cross_send.at[hop - 1],
            recv_sem=cross_recv.at[hop - 1],
            device_id={"clus": far(hop, core)},
            device_id_type=MESH,
        )

    own = pl.ds(pl.multiple_of(me * tall, tall), tall)

    def sum_copy(d):
        return pltpu.make_async_remote_copy(
            src_ref=summed,
            dst_ref=gram.at[own],
            send_sem=ag_send.at[d],
            recv_sem=ag_recv.at[d],
            device_id=device(d),
            device_id_type=MESH,
        )

    others = range(len(steps))
    add_gram(0, variables)
    pl.semaphore_wait(barrier, len(steps) + len(away))
    for d in others:
        part_copy(d).start()

    for copy in small:
        copy.wait()
    label_row = labels_ref[...]
    wide = jnp.broadcast_to(label_row.astype(jnp.float32), (count, count))
    same = (wide == wide.T).astype(jnp.bfloat16)
    before = lax.broadcasted_iota(jnp.int32, (count, count), 0) < lax.broadcasted_iota(
        jnp.int32, (count, count), 1
    )
    rank = dot(
        jnp.ones((16, count), jnp.bfloat16),
        jnp.where(before, same.astype(jnp.float32), 0.0).astype(jnp.bfloat16),
    )[:1].astype(jnp.int32)
    slots = lax.broadcasted_iota(jnp.int32, (room, count), 0)

    def pick(cluster):
        return jnp.where((slots == rank) & (label_row == cluster), 1.0, 0.0)

    def early_copy(slot, e):
        hop, c = away[slot]
        return pltpu.make_async_remote_copy(
            src_ref=packed.at[slot, e],
            dst_ref=got.at[(hop - 1) * CORES + core, e],
            send_sem=early_send.at[slot, e],
            recv_sem=early_recv.at[(hop - 1) * CORES + core, e],
            device_id={"clus": far(hop, c)},
            device_id_type=MESH,
        )

    def early_arrival(slot, e):
        return pltpu.make_async_remote_copy(
            src_ref=packed.at[slot, e],
            dst_ref=got.at[slot, e],
            send_sem=early_send.at[slot, e],
            recv_sem=early_recv.at[slot, e],
            device_id={"clus": far(*away[slot])},
            device_id_type=MESH,
        )

    def cells_of(u):
        return u // cuts, pl.ds(pl.multiple_of((u % cuts) * step, step), step)

    def spot(u, source):
        start = pl.multiple_of(source * width + (u % cuts) * step, step)
        return modes_ref.at[u // cuts, :, pl.ds(start, step)]

    picks = jnp.concatenate([pick(far(hop, c)) for hop, c in away], axis=0).astype(jnp.bfloat16)

    def send_early(low, high):
        @pl.loop(low, high)
        def _(e):
            v, cells = cells_of(late + e)
            made = dot(picks, snap[v, :, cells]).astype(jnp.bfloat16)
            for slot in range(len(away)):
                packed[slot, e] = made[slot * room : (slot + 1) * room]
            for slot in range(len(away)):
                early_copy(slot, e).start()

    send_early(0, 1)

    total = partial[own]
    for d in others:
        part_copy(d).wait_recv()
        total = total + landed[d]
    chunk[...] = total
    for hop in range(1, pairs):
        cross_copy(hop).start()
    send_early(1, 3)
    for hop in range(1, pairs):
        cross_copy(hop).wait_recv()
        total = total + crossed[hop - 1]
    total = total * (1.0 / (variables * width * devices))
    summed[...] = total
    gram[own] = total
    for d in others:
        sum_copy(d).start()
    send_early(3, early)
    for d in others:
        sum_copy(d).wait_recv()

    pieces = split3(gram[...])
    masked = jnp.concatenate([same * piece for piece in pieces], axis=1)
    basis = start_ref[...]
    for _ in range(ITERS):
        image = times_gram(basis, masked, count) + basis
        basis = orthonormal(image, same)

    keep = basis.astype(jnp.bfloat16).astype(jnp.float32)
    left = jnp.concatenate(
        [jnp.where(label_row == k, keep, 0.0) for k in range(clusters)], axis=0
    ).astype(jnp.bfloat16)

    def mode_copy(u, target, slot_out, slot_in):
        return pltpu.make_async_remote_copy(
            src_ref=stage.at[target, u],
            dst_ref=spot(u, owner),
            send_sem=out_send.at[u, slot_out],
            recv_sem=out_recv.at[u, slot_in],
            device_id={"clus": target},
            device_id_type=MESH,
        )

    def near_copy(u):
        return mode_copy(u, near, 0, 0)

    def far_copy(u, slot):
        hop, c = away[slot]
        return mode_copy(u, far(hop, c), 1 + slot, 1 + (hop - 1) * CORES + core)

    def far_arrival(u, slot):
        return mode_copy(u, far(*away[slot]), 1 + slot, 1 + slot)

    def own_copy(u):
        return pltpu.make_async_copy(stage.at[owner, u], spot(u, owner), own_sem.at[u])

    def grown_copy(slot, e):
        source = lax.rem(pair + pairs - away[slot][0], pairs) * CORES + away[slot][1]
        return pltpu.make_async_copy(
            grown.at[slot, e], spot(late + e, source), grown_sem.at[slot, e]
        )

    def make(u):
        v, cells = cells_of(u)
        made = dot(left, snap[v, :, cells]).astype(jnp.bfloat16)
        for k in range(clusters):
            stage[k, u] = made[k * modes : (k + 1) * modes]

    @pl.loop(0, late)
    def _(u):
        make(u)
        for slot in range(len(away)):
            far_copy(u, slot).start()
        near_copy(u).start()
        own_copy(u).start()

    @pl.loop(late, units)
    def _(u):
        make(u)
        near_copy(u).start()
        own_copy(u).start()

    share = coef_ref.shape[1]
    picked = jnp.zeros((modes, share), jnp.float32)
    for k in range(clusters):
        picked = jnp.where(owner == k, basis[:, k * share : (k + 1) * share], picked)
    coef_ref[...] = picked
    is_own = lax.broadcasted_iota(jnp.int32, (1, clusters), 1) == owner
    follower = jnp.sum(jnp.where(is_own, succ_ref[...], 0), axis=1, keepdims=True)
    mine = jnp.where(label_row == owner, keep, 0.0)
    other = jnp.where(label_row == follower, keep, 0.0).astype(jnp.bfloat16)
    parts = dot(other, jnp.concatenate(pieces, axis=1))
    image = parts[:, 2 * count :] + parts[:, count : 2 * count] + parts[:, :count]
    corr_ref[...] = lax.dot_general(
        mine,
        image,
        (((1,), (1,)), ((), ())),
        precision=lax.Precision.HIGHEST,
        preferred_element_type=jnp.float32,
    )

    compact = lax.dot_general(
        mine.astype(jnp.bfloat16),
        pick(owner).astype(jnp.bfloat16),
        (((1,), (1,)), ((), ())),
        preferred_element_type=jnp.float32,
    ).astype(jnp.bfloat16)

    @pl.loop(0, early)
    def _(e):
        for slot in range(len(away)):
            early_arrival(slot, e).wait_recv()
            grown[slot, e] = dot(compact, got[slot, e]).astype(jnp.bfloat16)
            grown_copy(slot, e).start()

    for hop in range(1, pairs):
        cross_copy(hop).wait_send()
    for d in others:
        part_copy(d).wait_send()
        sum_copy(d).wait_send()

    @pl.loop(0, early)
    def _(e):
        for slot in range(len(away)):
            early_copy(slot, e).wait_send()
            grown_copy(slot, e).wait()

    @pl.loop(late, units)
    def _(u):
        own_copy(u).wait()
        near_copy(u).wait()

    @pl.loop(0, late)
    def _(u):
        own_copy(u).wait()
        near_copy(u).wait()
        for slot in range(len(away)):
            far_copy(u, slot).wait_send()
            far_arrival(u, slot).wait_recv()


def write(*refs):
    inputs, outputs, held, read_sem, write_sem = refs[:3], refs[3:6], refs[6:9], *refs[9:]
    variables = inputs[0].shape[0]
    parts = [(0, v) for v in range(variables)] + [(1, None), (2, None)]

    def piece(arrays, part):
        ref = arrays[part[0]]
        return ref if part[1] is None else ref.at[part[1]]

    reads = [
        pltpu.make_async_copy(piece(inputs, part), piece(held, part), read_sem.at[i])
        for i, part in enumerate(parts)
    ]
    writes = [
        pltpu.make_async_copy(piece(held, part), piece(outputs, part), write_sem.at[i])
        for i, part in enumerate(parts)
    ]
    for copy in reads:
        copy.start()
    for read, copy in zip(reads, writes):
        read.wait()
        copy.start()
    for copy in writes:
        copy.wait()


def local(snapshots, labels, start, successor):
    count, variables, width = snapshots.shape
    spaces = lax.axis_size("space")
    clusters = lax.axis_size("clus")
    modes = start.shape[1]
    plane = spaces * CORES
    pairs = clusters // CORES
    tall = count // plane
    share = count // clusters
    room = CAP * clusters
    cuts = 3
    units, step = variables * cuts, width // cuts
    away = clusters - CORES
    vmem = pl.BlockSpec(memory_space=pltpu.VMEM)
    hbm = pl.BlockSpec(memory_space=pltpu.HBM)
    dma = pltpu.SemaphoreType.DMA
    results = (
        jax.ShapeDtypeStruct((variables, modes, clusters * width), jnp.bfloat16),
        jax.ShapeDtypeStruct((modes, share), jnp.float32),
        jax.ShapeDtypeStruct((modes, modes), jnp.float32),
    )
    made = pl.pallas_call(
        functools.partial(kernel, (spaces, clusters)),
        out_shape=results,
        in_specs=[hbm] * 4,
        out_specs=(hbm, vmem, vmem),
        scratch_shapes=[
            pltpu.VMEM((variables, count, width), jnp.bfloat16),
            pltpu.VMEM((1, count), jnp.int32),
            pltpu.VMEM((modes, count), jnp.float32),
            pltpu.VMEM((1, clusters), jnp.int32),
            pltpu.VMEM((count, count), jnp.float32),
            pltpu.VMEM((pairs - 1, tall, count), jnp.float32),
            pltpu.VMEM((tall, count), jnp.float32),
            pltpu.VMEM((plane, tall, count), jnp.float32),
            pltpu.VMEM((tall, count), jnp.float32),
            pltpu.VMEM((count, count), jnp.float32),
            pltpu.VMEM((clusters, units, modes, step), jnp.bfloat16),
            pltpu.VMEM((away, EARLY, room, step), jnp.bfloat16),
            pltpu.VMEM((away, EARLY, room, step), jnp.bfloat16),
            pltpu.VMEM((away, EARLY, modes, step), jnp.bfloat16),
            dma((variables,)),
            dma((3,)),
            dma((pairs - 1,)),
            dma((pairs - 1,)),
            dma((plane,)),
            dma((plane,)),
            dma((plane,)),
            dma((plane,)),
            dma((units, clusters)),
            dma((units, clusters)),
            dma((away, EARLY)),
            dma((away, EARLY)),
            dma((units,)),
            dma((away, EARLY)),
        ],
        compiler_params=pltpu.CompilerParams(
            collective_id=0, has_side_effects=True, vmem_limit_bytes=VMEM
        ),
    )(
        jnp.transpose(snapshots, (1, 0, 2)),
        labels.reshape(1, count),
        start.T,
        successor.reshape(1, clusters),
    )
    modes_out, coef, corr = pl.pallas_call(
        write,
        out_shape=results,
        in_specs=[hbm] * 3,
        out_specs=(hbm,) * 3,
        scratch_shapes=[pltpu.VMEM(x.shape, x.dtype) for x in results]
        + [dma((variables + 2,)), dma((variables + 2,))],
        compiler_params=pltpu.CompilerParams(vmem_limit_bytes=VMEM),
    )(*made)
    return jnp.transpose(modes_out, (1, 0, 2))[None], coef.T, corr[None]


def solution(mesh):
    in_specs = (P("groups", None, ("space", "clus")), P("groups"), P("groups", None), P("groups"))
    out_specs = (
        P(("groups", "clus"), None, None, "space"),
        P(("groups", "clus"), None),
        P(("groups", "clus"), None, None),
    )
    return jax.shard_map(local, mesh=mesh, in_specs=in_specs, out_specs=out_specs, check_vma=False)
```
